32 devices in a mesh: groups: 1, row: 8 (over z, y), col: 4 (over x, core), half: 1.
Axes of the slice: x: 2, y: 2, z: 4, core: 2. Of those that a mesh axis runs over, the one named last changes fastest.
Arguments:
- tokens: bfloat16 [4096, 1024], P(('groups', 'row', 'col'), 'half'), may hold values from -6 to 6
- expert_ids: int32 [4096, 8], P(('groups', 'row', 'col')), may hold values from 0 to 31, as said below
- gates: float32 [4096, 8], P(('groups', 'row', 'col')), may hold values from 0.02 to 0.4
- w_gate: bfloat16 [32, 1024, 512], P(('row', 'col'), None, 'half'), may hold values from -0.1875 to 0.1875
- w_up: bfloat16 [32, 1024, 512], P(('row', 'col'), None, 'half'), may hold values from -0.1875 to 0.1875
- w_down: bfloat16 [32, 512, 1024], P(('row', 'col'), 'half'), may hold values from -0.25 to 0.25
- grad_out: bfloat16 [4096, 1024], P(('groups', 'row', 'col'), 'half'), may hold values from -6 to 6
Outputs:
- mixed: bfloat16 [4096, 1024], P(('groups', 'row', 'col'), 'half')
- grad_tokens: bfloat16 [4096, 1024], P(('groups', 'row', 'col'), 'half')
- grad_gates: float32 [4096, 8], P(('groups', 'row', 'col'))
- grad_w_gate: bfloat16 [32, 1024, 512], P(('groups', 'row', 'col'), None, 'half')
- grad_w_up: bfloat16 [32, 1024, 512], P(('groups', 'row', 'col'), None, 'half')
- grad_w_down: bfloat16 [32, 512, 1024], P(('groups', 'row', 'col'), 'half')
The draws below stay inside these ranges and needn't reach their ends.
Inputs may be any that keep to these rules, and one draw needn't show every extreme that they name: `expert_ids`: the 8 experts of a token are distinct. Among the 128 tokens of each aligned block (the tokens of one index of row and col) no expert is named more than 48 times, and one expert, the same for all blocks, is named exactly 48 times in every block.
All inputs are finite; a program needn't handle non-finite values.
Results may differ from the reference program's by a relative error of at most 0.0071.
Values may be sent and summed in bfloat16 or wider, within the bound.
No kernel may reach another device: no remote copies, remote signals or barrier semaphores. Data moves between devices by JAX's collectives and lax.ppermute only.
A program may use at most 128 MiB of HBM per device.

```python
import math
import jax
import jax.numpy as jnp
from jax import lax

D = 1024
FF = 512
TOP = 8
TOK_DEV = 128
EXPERTS = 32
TOKENS = 4096
MOST = 48
N_ROW = 8
N_COL = 4
N_HALF = 1


def draw_expert_ids(key, part):
    key = jax.random.fold_in(key, 11)
    average = TOK_DEV * TOP // EXPERTS
    spread = MOST - average
    block_count = TOKENS // TOK_DEV
    hottest = jax.random.randint(jax.random.fold_in(key, 1), (), 0, EXPERTS).astype(jnp.int32)

    def one_block(block):
        block_key = jax.random.fold_in(key, block + 7)
        others = jax.random.permutation(jax.random.fold_in(block_key, 1), EXPERTS - 1).astype(jnp.int32) + 1
        order = (hottest + jnp.concatenate([jnp.zeros((1,), jnp.int32), others])) % EXPERTS
        shifts = jax.random.randint(jax.random.fold_in(block_key, 2), (EXPERTS // 2,), 0, spread + 1).astype(jnp.int32)
        shifts = shifts.at[0].set(spread)
        loads = jnp.stack([average + shifts, average - shifts], 1).reshape(EXPERTS)
        bounds = jnp.cumsum(loads)
        slots = jnp.arange(TOK_DEV * TOP, dtype=jnp.int32)
        placed = jnp.sum((slots[:, None] >= bounds[None, :]).astype(jnp.int32), 1)
        chosen = order[placed].reshape(TOP, TOK_DEV).T
        shuffle = jax.random.permutation(jax.random.fold_in(block_key, 3), TOK_DEV)
        return chosen[shuffle]
    blocks = jax.vmap(one_block)(jnp.arange(block_count, dtype=jnp.int32))
    return blocks.reshape(TOKENS, TOP).astype(jnp.int32)


def level_of(stream_key, dims, split, least, largest):
    def one(position, blocks):
        steps = jax.random.uniform(jax.random.fold_in(jax.random.fold_in(stream_key, 6), position), (blocks,), jnp.float32, least / len(split), largest / len(split))
        return jnp.repeat(jnp.exp(steps), dims[position] // blocks).reshape((-1,) + (1,) * (len(dims) - position - 1))

    gain = one(*split[0])
    for cut in split[1:]:
        gain = gain * one(*cut)
    return gain


def noise(own_key, dims, scale, reach, pieces=(), kind=jnp.bfloat16):
    result = scale * jax.random.normal(own_key, dims, jnp.float32)
    if pieces:
        result = result * level_of(own_key, dims, pieces, -0.22, 0.18)
    return jnp.clip(result, -reach, reach).astype(kind)


def setup_inputs(seed: int = 0, part: int = 0) -> dict:
    splits = jax.random.split(jax.random.key(seed), 8)
    own_keys = jax.random.split(jax.random.fold_in(splits[7], part), 8)
    tokens = noise(own_keys[0], (TOKENS, D), 1.0, 6.0, ((0, 32),))
    expert_ids = draw_expert_ids(jax.random.fold_in(jax.random.fold_in(splits[7], part), 71), part)
    gates = jnp.clip(jnp.exp(math.log(0.4) - 2.9957323 * jax.random.uniform(own_keys[2], (TOKENS, TOP), jnp.float32) ** level_of(own_keys[2], (TOKENS, TOP), ((0, 32),), -0.2, 0.2)), 0.02, 0.4)
    w_gate = noise(splits[3], (EXPERTS, D, FF), D ** -0.5, 0.1875, ((0, 32),))
    w_up = noise(splits[4], (EXPERTS, D, FF), D ** -0.5, 0.1875, ((0, 32),))
    w_down = noise(splits[5], (EXPERTS, FF, D), FF ** -0.5, 0.25, ((0, 32),))
    grad_out = noise(own_keys[6], (TOKENS, D), 1.0, 6.0, ((0, 32),))
    return {"tokens": tokens, "expert_ids": expert_ids, "gates": gates, "w_gate": w_gate, "w_up": w_up, "w_down": w_down, "grad_out": grad_out}


def reference(tokens, expert_ids, gates, w_gate, w_up, w_down, grad_out):
    entry_count = TOKENS * TOP
    capacity_all = N_ROW * N_COL * MOST
    share = FF // N_HALF
    flat_ids = expert_ids.reshape(entry_count)
    x_padded = jnp.concatenate([tokens, jnp.zeros((1, D), jnp.bfloat16)])
    dy_padded = jnp.concatenate([grad_out, jnp.zeros((1, D), jnp.bfloat16)])
    gate_padded = jnp.concatenate([gates.reshape(entry_count), jnp.zeros((1,), jnp.float32)])

    def per_expert(carry, expert):
        out_sum, grad_sum, gate_sum = carry
        entry_index = jnp.nonzero(flat_ids == expert, size=capacity_all, fill_value=entry_count)[0].astype(jnp.int32)
        token_rows = (entry_index // TOP).astype(jnp.int32)
        x_rows = x_padded[token_rows]
        dy_rows = dy_padded[token_rows]
        weight = gate_padded[entry_index]
        gate_mat = w_gate[expert]
        up_mat = w_up[expert]
        down_mat = w_down[expert]
        pre_gate = jnp.dot(x_rows, gate_mat, preferred_element_type=jnp.float32)
        pre_up = jnp.dot(x_rows, up_mat, preferred_element_type=jnp.float32)
        sigmoid_gate = jax.nn.sigmoid(pre_gate)
        act = (pre_gate * sigmoid_gate * pre_up).astype(jnp.bfloat16)
        out_total = jnp.zeros((capacity_all, D), jnp.float32)
        for portion in range(N_HALF):
            begin_at = portion * share
            end_at = begin_at + share
            partial_value = jnp.dot(act[:, begin_at:end_at], down_mat[begin_at:end_at], preferred_element_type=jnp.float32)
            out_total = out_total + lax.optimization_barrier(partial_value.astype(jnp.bfloat16)).astype(jnp.float32)
        out_total = lax.optimization_barrier(out_total.astype(jnp.bfloat16)).astype(jnp.float32)
        grad_routed = (weight[:, None] * dy_rows.astype(jnp.float32)).astype(jnp.bfloat16)
        grad_act = jnp.dot(grad_routed, down_mat.T, preferred_element_type=jnp.float32)
        grad_pre_gate = (grad_act * pre_up * sigmoid_gate * (1.0 + pre_gate * (1.0 - sigmoid_gate))).astype(jnp.bfloat16)
        grad_pre_up = (grad_act * pre_gate * sigmoid_gate).astype(jnp.bfloat16)
        dx_total = jnp.zeros((capacity_all, D), jnp.float32)
        for portion in range(N_HALF):
            begin_at = portion * share
            end_at = begin_at + share
            partial_value = jnp.dot(grad_pre_gate[:, begin_at:end_at], gate_mat[:, begin_at:end_at].T, preferred_element_type=jnp.float32)
            partial_value = partial_value + jnp.dot(grad_pre_up[:, begin_at:end_at], up_mat[:, begin_at:end_at].T, preferred_element_type=jnp.float32)
            dx_total = dx_total + lax.optimization_barrier(partial_value.astype(jnp.bfloat16)).astype(jnp.float32)
        dx_total = lax.optimization_barrier(dx_total.astype(jnp.bfloat16)).astype(jnp.float32)
        out_sum = out_sum.at[token_rows].add(weight[:, None] * out_total, mode="drop")
        grad_sum = grad_sum.at[token_rows].add(dx_total, mode="drop")
        gate_terms = jnp.sum(dy_rows.astype(jnp.float32) * out_total, 1)
        gate_sum = gate_sum.at[entry_index].add(gate_terms, mode="drop")
        grad_gate_mat = jnp.dot(x_rows.T, grad_pre_gate, preferred_element_type=jnp.float32).astype(jnp.bfloat16)
        grad_up_mat = jnp.dot(x_rows.T, grad_pre_up, preferred_element_type=jnp.float32).astype(jnp.bfloat16)
        grad_down_mat = jnp.dot(act.T, grad_routed, preferred_element_type=jnp.float32).astype(jnp.bfloat16)
        return (out_sum, grad_sum, gate_sum), (grad_gate_mat, grad_up_mat, grad_down_mat)

    start = (jnp.zeros((TOKENS, D), jnp.float32), jnp.zeros((TOKENS, D), jnp.float32), jnp.zeros((entry_count,), jnp.float32))
    final, stacked = lax.scan(per_expert, start, jnp.arange(EXPERTS, dtype=jnp.int32))
    out_sum, grad_sum, gate_sum = final
    mixed = out_sum.astype(jnp.bfloat16)
    grad_tokens = grad_sum.astype(jnp.bfloat16)
    grad_gates = gate_sum.reshape(TOKENS, TOP)
    return mixed, grad_tokens, grad_gates, stacked[0], stacked[1], stacked[2]
```

```python
import functools

import jax
import jax.numpy as jnp
from jax import lax
from jax.experimental import pallas as pl
from jax.experimental.pallas import tpu as pltpu
from jax.sharding import PartitionSpec as P


def padded_rows(source, slot_token):
    extended = jnp.concatenate([source, jnp.zeros((1, source.shape[1]), source.dtype)])
    return extended[slot_token]


def dispatch_rows(x_block, grad_block):
    return (
        lax.all_to_all(x_block, ("row", "col"), split_axis=0, concat_axis=0, tiled=True),
        lax.all_to_all(grad_block, ("row", "col"), split_axis=0, concat_axis=0, tiled=True),
    )


def return_outputs(block):
    return lax.all_to_all(block, ("row", "col"), split_axis=0, concat_axis=0, tiled=True)


def return_grads(block):
    return lax.all_to_all(block, ("row", "col"), split_axis=0, concat_axis=0, tiled=True)


def partner_total(moved):
    return jnp.sum(moved.astype(jnp.float32), 1).astype(jnp.bfloat16)


def local_exchange(tokens, expert_ids, gates, w_gate, w_up, w_down, grad_out):
    token_count, top_count = expert_ids.shape
    expert_count = lax.axis_size("row") * lax.axis_size("col")
    half_count = lax.axis_size("half")
    average = token_count * top_count // expert_count
    capacity = min(token_count, average + average // 2)
    entry_count = token_count * top_count
    flat_ids = expert_ids.reshape(entry_count)
    expert_range = jnp.arange(expert_count, dtype=jnp.int32)
    entry_hot = (expert_ids[:, :, None] == expert_range[None, None, :]).astype(jnp.float32)
    token_hot = jnp.sum(entry_hot, 1).astype(jnp.bfloat16)
    token_range = jnp.arange(token_count, dtype=jnp.int32)
    lower = (token_range[:, None] > token_range[None, :]).astype(jnp.bfloat16)
    before = jnp.dot(lower, token_hot, preferred_element_type=jnp.float32)
    earlier = jnp.sum(before[:, None, :] * entry_hot, 2).reshape(entry_count).astype(jnp.int32)
    position = flat_ids * capacity + earlier
    slot_entry = (
        jnp.full((expert_count * capacity,), entry_count, jnp.int32)
        .at[position]
        .set(jnp.arange(entry_count, dtype=jnp.int32))
    )
    slot_token = slot_entry // top_count
    gate_flat = jnp.concatenate([gates.reshape(entry_count), jnp.zeros((1,), jnp.float32)])
    slot_gate = gate_flat[slot_entry]
    x_source = lax.all_gather(tokens, "half", axis=1, tiled=True)
    dy_source = lax.all_gather(grad_out, "half", axis=1, tiled=True)
    x_send = padded_rows(x_source, slot_token)
    grad_send = (
        slot_gate[:, None] * padded_rows(dy_source, slot_token).astype(jnp.float32)
    ).astype(jnp.bfloat16)
    block_shape = (expert_count, capacity, x_send.shape[1])
    x_recv, grad_recv = dispatch_rows(x_send.reshape(block_shape), grad_send.reshape(block_shape))
    width = x_recv.shape[2]
    own_width = width // half_count
    row_total = expert_count * capacity
    x_rows = x_recv.reshape(row_total, width)
    grad_rows = grad_recv.reshape(row_total, width)
    gate_mat = w_gate[0]
    up_mat = w_up[0]
    down_mat = w_down[0]
    pre_gate = jnp.dot(x_rows, gate_mat, preferred_element_type=jnp.float32)
    pre_up = jnp.dot(x_rows, up_mat, preferred_element_type=jnp.float32)
    sigmoid_gate = jax.nn.sigmoid(pre_gate)
    act = (pre_gate * sigmoid_gate * pre_up).astype(jnp.bfloat16)
    partial_out = jnp.dot(act, down_mat, preferred_element_type=jnp.float32).astype(jnp.bfloat16)
    out_back = return_outputs(partial_out.reshape(expert_count, capacity, width))
    contract_last = (((1,), (1,)), ((), ()))
    contract_rows = (((0,), (0,)), ((), ()))
    grad_act = lax.dot_general(
        grad_rows, down_mat, contract_last, preferred_element_type=jnp.float32
    )
    grad_pre_gate = (
        grad_act * pre_up * sigmoid_gate * (1.0 + pre_gate * (1.0 - sigmoid_gate))
    ).astype(jnp.bfloat16)
    grad_pre_up = (grad_act * pre_gate * sigmoid_gate).astype(jnp.bfloat16)
    partial_grad = lax.dot_general(
        grad_pre_gate, gate_mat, contract_last, preferred_element_type=jnp.float32
    )
    partial_grad = (
        partial_grad
        + lax.dot_general(grad_pre_up, up_mat, contract_last, preferred_element_type=jnp.float32)
    ).astype(jnp.bfloat16)
    grad_back = return_grads(partial_grad.reshape(expert_count, capacity, width))
    grad_gate_mat = lax.dot_general(
        x_rows, grad_pre_gate, contract_rows, preferred_element_type=jnp.float32
    )
    grad_up_mat = lax.dot_general(
        x_rows, grad_pre_up, contract_rows, preferred_element_type=jnp.float32
    )
    grad_down_mat = lax.dot_general(
        act, grad_rows, contract_rows, preferred_element_type=jnp.float32
    )
    back_width = out_back.shape[2]
    routed_out = out_back.reshape(row_total, back_width)[position]
    routed_grad = grad_back.reshape(row_total, back_width)[position]
    split_shape = (entry_count, half_count, own_width)
    moved_out, moved_grad = (
        lax.all_to_all(
            routed_out.reshape(split_shape), "half", split_axis=1, concat_axis=1, tiled=True
        ),
        lax.all_to_all(
            routed_grad.reshape(split_shape), "half", split_axis=1, concat_axis=1, tiled=True
        ),
    )
    expert_out = partner_total(moved_out)
    expert_grad = partner_total(moved_grad)
    expert_out = expert_out.reshape(token_count, top_count, own_width).astype(jnp.float32)
    expert_grad = expert_grad.reshape(token_count, top_count, own_width).astype(jnp.float32)
    mixed = jnp.sum(gates[:, :, None] * expert_out, 1).astype(jnp.bfloat16)
    gate_terms = jnp.sum(grad_out.astype(jnp.float32)[:, None, :] * expert_out, 2)
    grad_gates = lax.psum(gate_terms, "half")
    grad_tokens = jnp.sum(expert_grad, 1).astype(jnp.bfloat16)
    return (
        mixed,
        grad_tokens,
        grad_gates,
        grad_gate_mat.astype(jnp.bfloat16)[None],
        grad_up_mat.astype(jnp.bfloat16)[None],
        grad_down_mat.astype(jnp.bfloat16)[None],
    )


META = 16
LEADING = (((0,), (0,)), ((), ()))
TRAILING = (((1,), (1,)), ((), ()))
CHIPS = 4
VMEM = pl.BlockSpec(memory_space=pltpu.VMEM)
SMEM = pl.BlockSpec(memory_space=pltpu.SMEM)


def plane_fits(mesh):
    size = mesh.shape
    return size["groups"] == 1 and size["half"] == 1 and size["col"] == 4 and size["row"] % 2 == 0 and size["row"] <= 32


def dot(left, right, dims=(((1,), (0,)), ((), ()))):
    return lax.dot_general(left, right, dims, preferred_element_type=jnp.float32)


def call(kernel, name, outs, in_specs, flops=0, moved=0, grid=()):
    return pl.pallas_call(
        kernel,
        out_shape=outs,
        grid=grid,
        in_specs=in_specs,
        out_specs=[VMEM] * len(outs),
        compiler_params=pltpu.CompilerParams(vmem_limit_bytes=56 * 1024 * 1024),
        cost_estimate=pl.CostEstimate(flops=flops, bytes_accessed=moved, transcendentals=0),
        name=name,
    )


def split_parts(value):
    first = value.astype(jnp.bfloat16)
    rest = value - first.astype(jnp.float32)
    second = rest.astype(jnp.bfloat16)
    third = (rest - second.astype(jnp.float32)).astype(jnp.bfloat16)
    return first, second, third


def store_meta(ref, pieces):
    tokens = pieces[0].shape[1]
    base = ref.shape[0] - META
    ref[base:, :] = jnp.zeros((META, ref.shape[1]), jnp.bfloat16)
    for number, piece in enumerate(pieces):
        piece = piece.astype(jnp.float32)
        missing = META - piece.shape[0]
        if missing:
            piece = jnp.concatenate([piece, jnp.zeros((missing, tokens), jnp.float32)], 0)
        ref[base:, number * tokens : (number + 1) * tokens] = piece.astype(jnp.bfloat16)


def load_meta(ref, tokens, number):
    base = ref.shape[0] - META
    return ref[base:, number * tokens : (number + 1) * tokens].astype(jnp.float32)


def join_kernel(tokens_ref, grad_ref, ids_ref, gates_ref, block_ref):
    tokens = tokens_ref.shape[0]
    block_ref[:tokens, :] = tokens_ref[...]
    block_ref[tokens : 2 * tokens, :] = grad_ref[...]
    store_meta(block_ref, (ids_ref[...].astype(jnp.float32).astype(jnp.bfloat16),) + split_parts(gates_ref[...]))


def selection(table_ref, block_ref, tokens, capacity, top):
    ids = load_meta(block_ref, tokens, 0)
    gates = load_meta(block_ref, tokens, 1) + load_meta(block_ref, tokens, 2) + load_meta(block_ref, tokens, 3)
    experts = [table_ref[place].astype(jnp.float32) for place in range(2 * CHIPS)]
    live = lax.broadcasted_iota(jnp.int32, ids.shape, 0) < top
    named = [(ids == expert) & live for expert in experts]
    hits = jnp.concatenate([jnp.sum(jnp.where(hit, 1.0, 0.0), 0, keepdims=True) for hit in named], 0)
    weights = [jnp.sum(jnp.where(hit, gates, 0.0), 0, keepdims=True) for hit in named]
    row = lax.broadcasted_iota(jnp.int32, (tokens, tokens), 0)
    column = lax.broadcasted_iota(jnp.int32, (tokens, tokens), 1)
    earlier = dot(hits.astype(jnp.bfloat16), jnp.where(row < column, 1.0, 0.0).astype(jnp.bfloat16))
    slot = lax.broadcasted_iota(jnp.int32, (capacity, tokens), 0).astype(jnp.float32)
    chosen = [
        jnp.where((slot == earlier[place : place + 1]) & (hits[place : place + 1] > 0.0), 1.0, 0.0)
        for place in range(2 * CHIPS)
    ]
    return chosen, weights, named


def pack_kernel(tokens, capacity, top, table_ref, block_ref, *out_refs):
    chosen, weights, _ = selection(table_ref, block_ref, tokens, capacity, top)
    stacked = jnp.concatenate(chosen, 0).astype(jnp.bfloat16)
    slot_gate = jnp.concatenate(
        [jnp.sum(pick * weight, 1, keepdims=True) for pick, weight in zip(chosen, weights)], 0
    )
    rows = dot(stacked, block_ref[:tokens, :]).astype(jnp.bfloat16)
    grads = (slot_gate * dot(stacked, block_ref[tokens : 2 * tokens, :])).astype(jnp.bfloat16)
    for place in range(2 * CHIPS):
        part = slice(place * capacity, (place + 1) * capacity)
        out_refs[place // 2][place % 2, :capacity, :] = rows[part]
        out_refs[place // 2][place % 2, capacity:, :] = grads[part]


def expert_kernel(capacity, *refs):
    own_refs, partner_ref = refs[:CHIPS], refs[CHIPS]
    gate_ref, up_ref, down_ref = refs[CHIPS + 1 : CHIPS + 4]
    own_out, partner_out, rows_ref, grads_ref, act_ref, pre_gate_ref, pre_up_ref = refs[CHIPS + 4 :]
    pieces = [ref[0] for ref in own_refs] + [partner_ref[chip] for chip in range(CHIPS)]
    rows = jnp.concatenate([piece[:capacity] for piece in pieces], 0)
    grads = jnp.concatenate([piece[capacity:] for piece in pieces], 0)
    rows_ref[...] = rows
    grads_ref[...] = grads
    pre_gate = dot(rows, gate_ref[...])
    pre_up = dot(rows, up_ref[...])
    sigmoid_gate = jax.nn.sigmoid(pre_gate)
    act = (pre_gate * sigmoid_gate * pre_up).astype(jnp.bfloat16)
    act_ref[...] = act
    out = dot(act, down_ref[...]).astype(jnp.bfloat16)
    grad_act = dot(grads, down_ref[...], TRAILING)
    grad_pre_gate = (
        grad_act * pre_up * sigmoid_gate * (1.0 + pre_gate * (1.0 - sigmoid_gate))
    ).astype(jnp.bfloat16)
    grad_pre_up = (grad_act * pre_gate * sigmoid_gate).astype(jnp.bfloat16)
    pre_gate_ref[...] = grad_pre_gate
    pre_up_ref[...] = grad_pre_up
    grad_in = (dot(grad_pre_gate, gate_ref[...], TRAILING) + dot(grad_pre_up, up_ref[...], TRAILING)).astype(
        jnp.bfloat16
    )
    for number in range(2 * CHIPS):
        part = slice(number * capacity, (number + 1) * capacity)
        target = own_out if number < CHIPS else partner_out
        target[number % CHIPS, :capacity, :] = out[part]
        target[number % CHIPS, capacity:, :] = grad_in[part]


def merge_kernel(tokens, capacity, top, table_ref, block_ref, own_ref, swapped_ref, *refs):
    back_refs, result_ref = refs[:-1], refs[-1]
    chosen, weights, named = selection(table_ref, block_ref, tokens, capacity, top)
    pieces = [own_ref[0], swapped_ref[0]] + [ref[core] for ref in back_refs for core in range(2)]
    out = jnp.concatenate([piece[:capacity] for piece in pieces], 0)
    grad = jnp.concatenate([piece[capacity:] for piece in pieces], 0)
    stacked = jnp.concatenate(chosen, 0).astype(jnp.bfloat16)
    weighted = jnp.concatenate([pick * weight for pick, weight in zip(chosen, weights)], 0)
    high, low, _ = split_parts(weighted)
    result_ref[:tokens, :] = (dot(high, out, LEADING) + dot(low, out, LEADING)).astype(jnp.bfloat16)
    result_ref[tokens : 2 * tokens, :] = dot(stacked, grad, LEADING).astype(jnp.bfloat16)
    source = dot(stacked, block_ref[tokens : 2 * tokens, :])
    terms = jnp.sum(source * out.astype(jnp.float32), 1, keepdims=True)
    total = jnp.zeros(named[0].shape, jnp.float32)
    for place in range(2 * CHIPS):
        part = slice(place * capacity, (place + 1) * capacity)
        per_token = jnp.sum(chosen[place] * terms[part], 0, keepdims=True)
        total = total + jnp.where(named[place], per_token, 0.0)
    store_meta(result_ref, split_parts(total))


def total_kernel(*refs):
    parts, (mixed_ref, grad_ref, gates_ref) = refs[:-3], refs[-3:]
    tokens = mixed_ref.shape[0]
    mixed = parts[0][:tokens, :].astype(jnp.float32)
    grad = parts[0][tokens : 2 * tokens, :].astype(jnp.float32)
    for part in parts[1:]:
        mixed = mixed + part[:tokens, :].astype(jnp.float32)
        grad = grad + part[tokens : 2 * tokens, :].astype(jnp.float32)
    mixed_ref[...] = mixed.astype(jnp.bfloat16)
    grad_ref[...] = grad.astype(jnp.bfloat16)
    gates = sum(load_meta(part, tokens, number) for part in parts for number in range(3))
    gates_ref[...] = gates[: gates_ref.shape[0]]


def weight_kernel(*refs):
    parts, (gate_ref, up_ref, down_ref) = refs[:-3], refs[-3:]
    steps = [parts[number : number + 5] for number in range(0, len(parts), 5)]
    gate_ref[...] = sum(dot(rows[...], gate[...], LEADING) for rows, _, _, gate, _ in steps).astype(jnp.bfloat16)
    up_ref[...] = sum(dot(rows[...], up[...], LEADING) for rows, _, _, _, up in steps).astype(jnp.bfloat16)
    down_ref[...] = sum(dot(act[...], grads[...], LEADING) for _, grads, act, _, _ in steps).astype(jnp.bfloat16)


def local_plane(tokens, expert_ids, gates, w_gate, w_up, w_down, grad_out):
    token_count, top_count = expert_ids.shape
    width = tokens.shape[1]
    hidden = w_gate.shape[2]
    axes = ("row", "col")
    plane = 2 * CHIPS
    device_count = lax.axis_size("row") * lax.axis_size("col")
    levels = device_count // plane
    average = token_count * top_count // device_count
    capacity = -(-min(token_count, average + average // 2) // 16) * 16
    me = lax.axis_index("row") * lax.axis_size("col") + lax.axis_index("col")
    table = (me // plane) * plane + jnp.bitwise_xor(me % plane, jnp.arange(plane, dtype=jnp.int32))
    bf16 = functools.partial(jax.ShapeDtypeStruct, dtype=jnp.bfloat16)

    def flip(value, mask):
        pairs = [(device, device ^ mask) for device in range(device_count)]
        return lax.ppermute(value, axes, pairs)

    def climb(value, step):
        pairs = [(device, (device + step * plane) % device_count) for device in range(device_count)]
        return lax.ppermute(value, axes, pairs)

    block_rows = 2 * token_count + META
    row_total = plane * capacity
    pair = bf16((2, 2 * capacity, width))
    quad = bf16((CHIPS, 2 * capacity, width))
    (block,) = call(join_kernel, "join", [bf16((block_rows, width))], [VMEM] * 4, 0, 4 * block_rows * width)(
        tokens, grad_out, expert_ids.T, gates.T
    )
    order = [0] + sorted(range(1, levels), key=lambda step: min(step, levels - step))
    blocks = {step: climb(block, step) if step else block for step in order}
    pack = call(
        functools.partial(pack_kernel, token_count, capacity, top_count),
        "pack",
        [pair] * CHIPS,
        [SMEM, VMEM],
        4 * row_total * token_count * width,
        2 * (block_rows + 2 * row_total) * width,
    )
    first = pl.BlockSpec((1, 2 * capacity, width), lambda step: (0, 0, 0), memory_space=pltpu.VMEM)
    expert = call(
        functools.partial(expert_kernel, capacity),
        "expert",
        [quad, quad, bf16((row_total, width)), bf16((row_total, width))] + [bf16((row_total, hidden))] * 3,
        [first] * CHIPS + [VMEM] * 4,
        12 * row_total * width * hidden,
        2 * (6 * row_total * width + 3 * row_total * hidden + 3 * width * hidden),
        (1,),
    )
    merge = call(
        functools.partial(merge_kernel, token_count, capacity, top_count),
        "merge",
        [bf16((block_rows, width))],
        [SMEM, VMEM, first, first] + [VMEM] * (CHIPS - 1),
        8 * row_total * token_count * width,
        2 * (2 * block_rows + 2 * row_total) * width,
        (1,),
    )
    saved = []
    finished = {}
    for step in order:
        packed = pack(table, blocks[step])
        arrived = [packed[0]] + [flip(packed[chip], 2 * chip) for chip in range(1, CHIPS)]
        swapped = flip(jnp.stack([part[1] for part in arrived]), 1)
        own_out, partner_out, *kept = expert(*arrived, swapped, w_gate[0], w_up[0], w_down[0])
        saved.append(kept)
        back = flip(partner_out, 1)
        home = [flip(jnp.stack([own_out[chip], back[chip]]), 2 * chip) for chip in range(1, CHIPS)]
        (merged,) = merge(table, blocks[step], own_out, back, *home)
        finished[step] = climb(merged, levels - step) if step else merged
    half_block = bf16((token_count, width))
    mixed, grad_tokens, grad_gates = call(
        total_kernel,
        "total",
        [half_block, half_block, jax.ShapeDtypeStruct((top_count, token_count), jnp.float32)],
        [VMEM] * levels,
        0,
        2 * (levels + 1) * block_rows * width,
    )(*[finished[step] for step in order])
    grad_gate_mat, grad_up_mat, grad_down_mat = call(
        weight_kernel,
        "weight",
        [bf16((width, hidden)), bf16((width, hidden)), bf16((hidden, width))],
        [VMEM] * (5 * levels),
        6 * levels * row_total * width * hidden,
        2 * levels * row_total * (2 * width + 3 * hidden) + 6 * width * hidden,
    )(*[value for kept in saved for value in kept])
    return mixed, grad_tokens, grad_gates.T, grad_gate_mat[None], grad_up_mat[None], grad_down_mat[None]


def solution(mesh):
    return jax.shard_map(
        local_plane if plane_fits(mesh) else local_exchange,
        mesh=mesh,
        in_specs=(
            P(("groups", "row", "col"), "half"),
            P(("groups", "row", "col"), None),
            P(("groups", "row", "col"), None),
            P(("row", "col"), None, "half"),
            P(("row", "col"), None, "half"),
            P(("row", "col"), "half", None),
            P(("groups", "row", "col"), "half"),
        ),
        out_specs=(
            P(("groups", "row", "col"), "half"),
            P(("groups", "row", "col"), "half"),
            P(("groups", "row", "col"), None),
            P(("groups", "row", "col"), None, "half"),
            P(("groups", "row", "col"), None, "half"),
            P(("groups", "row", "col"), "half", None),
        ),
        check_vma=False,
    )
```

```python
import functools

import jax
import jax.numpy as jnp
from jax import lax
from jax.experimental import pallas as pl
from jax.experimental.pallas import tpu as pltpu
from jax.sharding import PartitionSpec as P


def padded_rows(source, slot_token):
    extended = jnp.concatenate([source, jnp.zeros((1, source.shape[1]), source.dtype)])
    return extended[slot_token]


def dispatch_rows(x_block, grad_block):
    return (
        lax.all_to_all(x_block, ("row", "col"), split_axis=0, concat_axis=0, tiled=True),
        lax.all_to_all(grad_block, ("row", "col"), split_axis=0, concat_axis=0, tiled=True),
    )


def return_outputs(block):
    return lax.all_to_all(block, ("row", "col"), split_axis=0, concat_axis=0, tiled=True)


def return_grads(block):
    return lax.all_to_all(block, ("row", "col"), split_axis=0, concat_axis=0, tiled=True)


def partner_total(moved):
    return jnp.sum(moved.astype(jnp.float32), 1).astype(jnp.bfloat16)


def local_exchange(tokens, expert_ids, gates, w_gate, w_up, w_down, grad_out):
    token_count, top_count = expert_ids.shape
    expert_count = lax.axis_size("row") * lax.axis_size("col")
    half_count = lax.axis_size("half")
    average = token_count * top_count // expert_count
    capacity = min(token_count, average + average // 2)
    entry_count = token_count * top_count
    flat_ids = expert_ids.reshape(entry_count)
    expert_range = jnp.arange(expert_count, dtype=jnp.int32)
    entry_hot = (expert_ids[:, :, None] == expert_range[None, None, :]).astype(jnp.float32)
    token_hot = jnp.sum(entry_hot, 1).astype(jnp.bfloat16)
    token_range = jnp.arange(token_count, dtype=jnp.int32)
    lower = (token_range[:, None] > token_range[None, :]).astype(jnp.bfloat16)
    before = jnp.dot(lower, token_hot, preferred_element_type=jnp.float32)
    earlier = jnp.sum(before[:, None, :] * entry_hot, 2).reshape(entry_count).astype(jnp.int32)
    position = flat_ids * capacity + earlier
    slot_entry = (
        jnp.full((expert_count * capacity,), entry_count, jnp.int32)
        .at[position]
        .set(jnp.arange(entry_count, dtype=jnp.int32))
    )
    slot_token = slot_entry // top_count
    gate_flat = jnp.concatenate([gates.reshape(entry_count), jnp.zeros((1,), jnp.float32)])
    slot_gate = gate_flat[slot_entry]
    x_source = lax.all_gather(tokens, "half", axis=1, tiled=True)
    dy_source = lax.all_gather(grad_out, "half", axis=1, tiled=True)
    x_send = padded_rows(x_source, slot_token)
    grad_send = (
        slot_gate[:, None] * padded_rows(dy_source, slot_token).astype(jnp.float32)
    ).astype(jnp.bfloat16)
    block_shape = (expert_count, capacity, x_send.shape[1])
    x_recv, grad_recv = dispatch_rows(x_send.reshape(block_shape), grad_send.reshape(block_shape))
    width = x_recv.shape[2]
    own_width = width // half_count
    row_total = expert_count * capacity
    x_rows = x_recv.reshape(row_total, width)
    grad_rows = grad_recv.reshape(row_total, width)
    gate_mat = w_gate[0]
    up_mat = w_up[0]
    down_mat = w_down[0]
    pre_gate = jnp.dot(x_rows, gate_mat, preferred_element_type=jnp.float32)
    pre_up = jnp.dot(x_rows, up_mat, preferred_element_type=jnp.float32)
    sigmoid_gate = jax.nn.sigmoid(pre_gate)
    act = (pre_gate * sigmoid_gate * pre_up).astype(jnp.bfloat16)
    partial_out = jnp.dot(act, down_mat, preferred_element_type=jnp.float32).astype(jnp.bfloat16)
    out_back = return_outputs(partial_out.reshape(expert_count, capacity, width))
    contract_last = (((1,), (1,)), ((), ()))
    contract_rows = (((0,), (0,)), ((), ()))
    grad_act = lax.dot_general(
        grad_rows, down_mat, contract_last, preferred_element_type=jnp.float32
    )
    grad_pre_gate = (
        grad_act * pre_up * sigmoid_gate * (1.0 + pre_gate * (1.0 - sigmoid_gate))
    ).astype(jnp.bfloat16)
    grad_pre_up = (grad_act * pre_gate * sigmoid_gate).astype(jnp.bfloat16)
    partial_grad = lax.dot_general(
        grad_pre_gate, gate_mat, contract_last, preferred_element_type=jnp.float32
    )
    partial_grad = (
        partial_grad
        + lax.dot_general(grad_pre_up, up_mat, contract_last, preferred_element_type=jnp.float32)
    ).astype(jnp.bfloat16)
    grad_back = return_grads(partial_grad.reshape(expert_count, capacity, width))
    grad_gate_mat = lax.dot_general(
        x_rows, grad_pre_gate, contract_rows, preferred_element_type=jnp.float32
    )
    grad_up_mat = lax.dot_general(
        x_rows, grad_pre_up, contract_rows, preferred_element_type=jnp.float32
    )
    grad_down_mat = lax.dot_general(
        act, grad_rows, contract_rows, preferred_element_type=jnp.float32
    )
    back_width = out_back.shape[2]
    routed_out = out_back.reshape(row_total, back_width)[position]
    routed_grad = grad_back.reshape(row_total, back_width)[position]
    split_shape = (entry_count, half_count, own_width)
    moved_out, moved_grad = (
        lax.all_to_all(
            routed_out.reshape(split_shape), "half", split_axis=1, concat_axis=1, tiled=True
        ),
        lax.all_to_all(
            routed_grad.reshape(split_shape), "half", split_axis=1, concat_axis=1, tiled=True
        ),
    )
    expert_out = partner_total(moved_out)
    expert_grad = partner_total(moved_grad)
    expert_out = expert_out.reshape(token_count, top_count, own_width).astype(jnp.float32)
    expert_grad = expert_grad.reshape(token_count, top_count, own_width).astype(jnp.float32)
    mixed = jnp.sum(gates[:, :, None] * expert_out, 1).astype(jnp.bfloat16)
    gate_terms = jnp.sum(grad_out.astype(jnp.float32)[:, None, :] * expert_out, 2)
    grad_gates = lax.psum(gate_terms, "half")
    grad_tokens = jnp.sum(expert_grad, 1).astype(jnp.bfloat16)
    return (
        mixed,
        grad_tokens,
        grad_gates,
        grad_gate_mat.astype(jnp.bfloat16)[None],
        grad_up_mat.astype(jnp.bfloat16)[None],
        grad_down_mat.astype(jnp.bfloat16)[None],
    )


META = 16
LEADING = (((0,), (0,)), ((), ()))
TRAILING = (((1,), (1,)), ((), ()))
CHIPS = 4
COST = {'join': 1.0, 'pack': 0, 'expert': 0, 'merge': 0, 'weight': 0}
WHEN = 0
FAR = 0
WPOS = 1
BEHIND = 1
STRICT = 0
AHEAD = 1
WEIGHT_A = 1
WEIGHT_B = 2
VMEM = pl.BlockSpec(memory_space=pltpu.VMEM)
SMEM = pl.BlockSpec(memory_space=pltpu.SMEM)


def plane_fits(mesh):
    size = mesh.shape
    return size["groups"] == 1 and size["half"] == 1 and size["col"] == 4 and size["row"] % 2 == 0 and size["row"] <= 32


def dot(left, right, dims=(((1,), (0,)), ((), ()))):
    return lax.dot_general(left, right, dims, preferred_element_type=jnp.float32)


def call(kernel, name, outs, in_specs, flops=0, moved=0, grid=()):
    used = len(in_specs)

    def ordered(*refs):
        kernel(*refs[:used], *refs[used + 1 :])

    return pl.pallas_call(
        ordered,
        out_shape=outs,
        grid=grid,
        in_specs=in_specs + [pl.BlockSpec(memory_space=pl.ANY)],
        out_specs=[VMEM] * len(outs),
        compiler_params=pltpu.CompilerParams(vmem_limit_bytes=56 * 1024 * 1024),
        cost_estimate=pl.CostEstimate(flops=int(flops * COST[name]), bytes_accessed=moved if COST[name] > 0.5 else 0, transcendentals=0),
        name=name,
    )


def split_parts(value):
    first = value.astype(jnp.bfloat16)
    rest = value - first.astype(jnp.float32)
    second = rest.astype(jnp.bfloat16)
    third = (rest - second.astype(jnp.float32)).astype(jnp.bfloat16)
    return first, second, third


def store_meta(ref, pieces):
    tokens = pieces[0].shape[1]
    base = ref.shape[0] - META
    ref[base:, :] = jnp.zeros((META, ref.shape[1]), jnp.bfloat16)
    for number, piece in enumerate(pieces):
        piece = piece.astype(jnp.float32)
        missing = META - piece.shape[0]
        if missing:
            piece = jnp.concatenate([piece, jnp.zeros((missing, tokens), jnp.float32)], 0)
        ref[base:, number * tokens : (number + 1) * tokens] = piece.astype(jnp.bfloat16)


def load_meta(ref, tokens, number):
    base = ref.shape[0] - META
    return ref[base:, number * tokens : (number + 1) * tokens].astype(jnp.float32)


def join_kernel(tokens_ref, grad_ref, ids_ref, gates_ref, block_ref):
    tokens = tokens_ref.shape[0]
    block_ref[:tokens, :] = tokens_ref[...]
    block_ref[tokens : 2 * tokens, :] = grad_ref[...]
    store_meta(block_ref, (ids_ref[...].astype(jnp.float32).astype(jnp.bfloat16),) + split_parts(gates_ref[...]))


def selection(table_ref, block_ref, tokens, capacity, top):
    ids = load_meta(block_ref, tokens, 0)
    gates = load_meta(block_ref, tokens, 1) + load_meta(block_ref, tokens, 2) + load_meta(block_ref, tokens, 3)
    experts = [table_ref[place].astype(jnp.float32) for place in range(2 * CHIPS)]
    live = lax.broadcasted_iota(jnp.int32, ids.shape, 0) < top
    named = [(ids == expert) & live for expert in experts]
    hits = jnp.concatenate([jnp.sum(jnp.where(hit, 1.0, 0.0), 0, keepdims=True) for hit in named], 0)
    weights = [jnp.sum(jnp.where(hit, gates, 0.0), 0, keepdims=True) for hit in named]
    row = lax.broadcasted_iota(jnp.int32, (tokens, tokens), 0)
    column = lax.broadcasted_iota(jnp.int32, (tokens, tokens), 1)
    earlier = dot(hits.astype(jnp.bfloat16), jnp.where(row < column, 1.0, 0.0).astype(jnp.bfloat16))
    slot = lax.broadcasted_iota(jnp.int32, (capacity, tokens), 0).astype(jnp.float32)
    chosen = [
        jnp.where((slot == earlier[place : place + 1]) & (hits[place : place + 1] > 0.0), 1.0, 0.0)
        for place in range(2 * CHIPS)
    ]
    return chosen, weights, named


def pack_kernel(tokens, capacity, top, table_ref, block_ref, *out_refs):
    chosen, weights, _ = selection(table_ref, block_ref, tokens, capacity, top)
    stacked = jnp.concatenate(chosen, 0).astype(jnp.bfloat16)
    slot_gate = jnp.concatenate(
        [jnp.sum(pick * weight, 1, keepdims=True) for pick, weight in zip(chosen, weights)], 0
    )
    rows = dot(stacked, block_ref[:tokens, :]).astype(jnp.bfloat16)
    grads = (slot_gate * dot(stacked, block_ref[tokens : 2 * tokens, :])).astype(jnp.bfloat16)
    for place in range(2 * CHIPS):
        part = slice(place * capacity, (place + 1) * capacity)
        out_refs[place // 2][place % 2, :capacity, :] = rows[part]
        out_refs[place // 2][place % 2, capacity:, :] = grads[part]


def expert_kernel(capacity, *refs):
    in_refs, weight_refs, out_refs = refs[:CHIPS], refs[CHIPS : CHIPS + 6], refs[CHIPS + 6 : 2 * CHIPS + 6]
    rows_ref, grads_ref, act_ref, pre_gate_ref, pre_up_ref = refs[2 * CHIPS + 6 :]
    for core in range(2):
        gate_ref, up_ref, down_ref = weight_refs[3 * core : 3 * core + 3]
        rows = jnp.concatenate([ref[core, :capacity] for ref in in_refs], 0)
        grads = jnp.concatenate([ref[core, capacity:] for ref in in_refs], 0)
        rows_ref[core] = rows
        grads_ref[core] = grads
        pre_gate = dot(rows, gate_ref[...])
        pre_up = dot(rows, up_ref[...])
        sigmoid_gate = jax.nn.sigmoid(pre_gate)
        act = (pre_gate * sigmoid_gate * pre_up).astype(jnp.bfloat16)
        act_ref[core] = act
        out = dot(act, down_ref[...]).astype(jnp.bfloat16)
        grad_act = dot(grads, down_ref[...], TRAILING)
        grad_pre_gate = (
            grad_act * pre_up * sigmoid_gate * (1.0 + pre_gate * (1.0 - sigmoid_gate))
        ).astype(jnp.bfloat16)
        grad_pre_up = (grad_act * pre_gate * sigmoid_gate).astype(jnp.bfloat16)
        pre_gate_ref[core] = grad_pre_gate
        pre_up_ref[core] = grad_pre_up
        grad_in = (
            dot(grad_pre_gate, gate_ref[...], TRAILING) + dot(grad_pre_up, up_ref[...], TRAILING)
        ).astype(jnp.bfloat16)
        for chip in range(CHIPS):
            part = slice(chip * capacity, (chip + 1) * capacity)
            out_refs[chip][core, :capacity, :] = out[part]
            out_refs[chip][core, capacity:, :] = grad_in[part]


def merge_kernel(tokens, capacity, top, before, table_ref, block_ref, *refs):
    back_refs, earlier_refs, out_refs = refs[:CHIPS], refs[CHIPS : CHIPS + before], refs[CHIPS + before :]
    chosen, weights, named = selection(table_ref, block_ref, tokens, capacity, top)
    pieces = [ref[core] for ref in back_refs for core in range(2)]
    out = jnp.concatenate([piece[:capacity] for piece in pieces], 0)
    grad = jnp.concatenate([piece[capacity:] for piece in pieces], 0)
    stacked = jnp.concatenate(chosen, 0).astype(jnp.bfloat16)
    weighted = jnp.concatenate([pick * weight for pick, weight in zip(chosen, weights)], 0)
    high, low, _ = split_parts(weighted)
    mixed = dot(high, out, LEADING) + dot(low, out, LEADING)
    grad_in = dot(stacked, grad, LEADING)
    source = dot(stacked, block_ref[tokens : 2 * tokens, :])
    terms = jnp.sum(source * out.astype(jnp.float32), 1, keepdims=True)
    total = jnp.zeros(named[0].shape, jnp.float32)
    for place in range(2 * CHIPS):
        part = slice(place * capacity, (place + 1) * capacity)
        per_token = jnp.sum(chosen[place] * terms[part], 0, keepdims=True)
        total = total + jnp.where(named[place], per_token, 0.0)
    for ref in earlier_refs:
        mixed = mixed + ref[:tokens, :].astype(jnp.float32)
        grad_in = grad_in + ref[tokens : 2 * tokens, :].astype(jnp.float32)
        total = total + sum(load_meta(ref, tokens, number) for number in range(3))
    if len(out_refs) == 1:
        out_refs[0][:tokens, :] = mixed.astype(jnp.bfloat16)
        out_refs[0][tokens : 2 * tokens, :] = grad_in.astype(jnp.bfloat16)
        store_meta(out_refs[0], split_parts(total))
    else:
        out_refs[0][...] = mixed.astype(jnp.bfloat16)
        out_refs[1][...] = grad_in.astype(jnp.bfloat16)
        out_refs[2][...] = total[:top]


def weight_kernel(levels, *refs):
    steps = [refs[number : number + 5] for number in range(0, 5 * levels, 5)]
    gate_mat = sum(dot(rows[0], gate[0], LEADING) for rows, _, _, gate, _ in steps)
    up_mat = sum(dot(rows[0], up[0], LEADING) for rows, _, _, _, up in steps)
    down_mat = sum(dot(act[0], grads[0], LEADING) for _, grads, act, _, _ in steps)
    width, hidden = gate_mat.shape
    if len(refs) == 5 * levels + 1:
        refs[-1][:width, :hidden] = gate_mat.astype(jnp.bfloat16)
        refs[-1][:width, hidden:] = up_mat.astype(jnp.bfloat16)
        refs[-1][width:, :] = down_mat.astype(jnp.bfloat16)
        return
    other_ref, (gate_ref, up_ref, down_ref) = refs[5 * levels], refs[-3:]
    gate_ref[...] = (gate_mat + other_ref[:width, :hidden].astype(jnp.float32)).astype(jnp.bfloat16)
    up_ref[...] = (up_mat + other_ref[:width, hidden:].astype(jnp.float32)).astype(jnp.bfloat16)
    down_ref[...] = (down_mat + other_ref[width:, :].astype(jnp.float32)).astype(jnp.bfloat16)


def local_plane(tokens, expert_ids, gates, w_gate, w_up, w_down, grad_out):
    token_count, top_count = expert_ids.shape
    width = tokens.shape[1]
    hidden = w_gate.shape[2]
    axes = ("row", "col")
    plane = 2 * CHIPS
    device_count = lax.axis_size("row") * lax.axis_size("col")
    levels = device_count // plane
    average = token_count * top_count // device_count
    capacity = -(-min(token_count, average + average // 2) // 16) * 16
    me = lax.axis_index("row") * lax.axis_size("col") + lax.axis_index("col")
    table = (me // plane) * plane + jnp.bitwise_xor(me % plane, jnp.arange(plane, dtype=jnp.int32))
    bf16 = functools.partial(jax.ShapeDtypeStruct, dtype=jnp.bfloat16)

    def flip(value, mask):
        pairs = [(device, device ^ mask) for device in range(device_count)]
        return lax.ppermute(value, axes, pairs)

    def climb(value, step):
        pairs = [(device, (device + step * plane) % device_count) for device in range(device_count)]
        return lax.ppermute(value, axes, pairs)

    block_rows = 2 * token_count + META
    row_total = plane * capacity
    pair = bf16((2, 2 * capacity, width))
    half_rows = row_total // 2
    (block,) = call(join_kernel, "join", [bf16((block_rows, width))], [VMEM] * 4, 0, 4 * block_rows * width)(
        tokens, grad_out, expert_ids.T, gates.T, gates
    )
    order = list(range(levels))
    pack = call(
        functools.partial(pack_kernel, token_count, capacity, top_count),
        "pack",
        [pair] * CHIPS,
        [SMEM, VMEM],
        4 * row_total * token_count * width,
        2 * (block_rows + 2 * row_total) * width,
    )
    kept_shapes = [bf16((2, half_rows, size)) for size in (width, width, hidden, hidden, hidden)]
    expert = call(
        functools.partial(expert_kernel, capacity),
        "expert",
        [pair] * CHIPS + kept_shapes,
        [VMEM] * (CHIPS + 6),
        12 * row_total * width * hidden,
        2 * (6 * row_total * width + 3 * row_total * hidden + 6 * width * hidden),
    )
    half_block = bf16((token_count, width))
    results_shapes = [half_block, half_block, jax.ShapeDtypeStruct((top_count, token_count), jnp.float32)]

    def merge(before, final):
        return call(
            functools.partial(merge_kernel, token_count, capacity, top_count, before),
            "merge",
            results_shapes if final else [bf16((block_rows, width))],
            [SMEM] + [VMEM] * (1 + CHIPS + before),
            8 * row_total * token_count * width,
            2 * (2 * block_rows + 2 * row_total) * width,
        )

    def weight(core, partials):
        specs = [
            pl.BlockSpec((1,) + shape.shape[1:], lambda step: (core, 0, 0), memory_space=pltpu.VMEM) for shape in kept_shapes
        ]
        return call(
            functools.partial(weight_kernel, levels),
            "weight",
            [bf16((width, hidden)), bf16((width, hidden)), bf16((hidden, width))]
            if partials
            else [bf16((width + hidden, 2 * hidden))],
            specs * levels + [VMEM] * partials,
            3 * levels * row_total * width * hidden,
            levels * row_total * (2 * width + 3 * hidden) + 6 * width * hidden,
            (1,),
        )

    def after(value, *earlier):
        return lax.optimization_barrier((value,) + earlier)[0]

    moved = []

    def exchange(parts):
        earlier = moved[-BEHIND] if len(moved) >= BEHIND else None
        received = [parts[0]]
        for chip in range(1, CHIPS):
            part = after(parts[chip], *(earlier[1:] if STRICT else earlier[chip : chip + 1])) if earlier else parts[chip]
            received.append(flip(part, 2 * chip))
        moved.append(received)
        return received

    mats = [w_gate[0], w_up[0], w_down[0]]
    blocks = {0: block}
    for step in order[1:]:
        blocks[step] = climb(block, step)
    arrived, results, kept = {}, {}, {}
    last = block
    for turn in range(levels + AHEAD):
        if turn == min(WHEN, levels - 1):
            for mat in mats[:3]:
                mats.append(flip(mat, 1))
            last = after(last, *mats[3:])
        if turn < levels:
            packed = pack(table, blocks[order[turn]], last)
            last = packed[0]
            arrived[order[turn]] = exchange(packed)
        if turn >= AHEAD:
            step = order[turn - AHEAD]
            outs = expert(*arrived[step], *mats, last)
            last = outs[0]
            results[step], kept[step] = outs[:CHIPS], outs[CHIPS:]
    homeward = (sorted(order[1:], key=lambda step: -min(step, levels - step)) if FAR else order[1:]) + order[:1]
    returned = {step: exchange(results[step]) for step in homeward}
    saved = [value for step in order for value in kept[step]]
    sent = []
    for turn, step in enumerate(homeward):
        if turn == WPOS:
            (partial,) = weight(1, 0)(*saved, last)
            last = partial
            partial = flip(partial, 1)
        if turn == levels - 1:
            grad_mats = weight(0, 1)(*saved, partial, last)
            last = grad_mats[0]
        earlier, final = (sent, True) if step == 0 else ([], False)
        merged = merge(len(earlier), final)(table, blocks[step], *returned[step], *earlier, last)
        last = merged[0]
        if step:
            sent.append(climb(merged[0], levels - step))
    mixed, grad_tokens, grad_gates = merged
    return (mixed, grad_tokens, grad_gates.T) + tuple(mat[None] for mat in grad_mats)


def solution(mesh):
    return jax.shard_map(
        local_plane if plane_fits(mesh) else local_exchange,
        mesh=mesh,
        in_specs=(
            P(("groups", "row", "col"), "half"),
            P(("groups", "row", "col"), None),
            P(("groups", "row", "col"), None),
            P(("row", "col"), None, "half"),
            P(("row", "col"), None, "half"),
            P(("row", "col"), "half", None),
            P(("groups", "row", "col"), "half"),
        ),
        out_specs=(
            P(("groups", "row", "col"), "half"),
            P(("groups", "row", "col"), "half"),
            P(("groups", "row", "col"), None),
            P(("groups", "row", "col"), None, "half"),
            P(("groups", "row", "col"), None, "half"),
            P(("groups", "row", "col"), "half", None),
        ),
        check_vma=False,
    )
```

```python
import functools

import jax
import jax.numpy as jnp
from jax import lax
from jax.experimental import pallas as pl
from jax.experimental.pallas import tpu as pltpu
from jax.sharding import PartitionSpec as P


def padded_rows(source, slot_token):
    extended = jnp.concatenate([source, jnp.zeros((1, source.shape[1]), source.dtype)])
    return extended[slot_token]


def dispatch_rows(x_block, grad_block):
    return (
        lax.all_to_all(x_block, ("row", "col"), split_axis=0, concat_axis=0, tiled=True),
        lax.all_to_all(grad_block, ("row", "col"), split_axis=0, concat_axis=0, tiled=True),
    )


def return_outputs(block):
    return lax.all_to_all(block, ("row", "col"), split_axis=0, concat_axis=0, tiled=True)


def return_grads(block):
    return lax.all_to_all(block, ("row", "col"), split_axis=0, concat_axis=0, tiled=True)


def partner_total(moved):
    return jnp.sum(moved.astype(jnp.float32), 1).astype(jnp.bfloat16)


def local_exchange(tokens, expert_ids, gates, w_gate, w_up, w_down, grad_out):
    token_count, top_count = expert_ids.shape
    expert_count = lax.axis_size("row") * lax.axis_size("col")
    half_count = lax.axis_size("half")
    average = token_count * top_count // expert_count
    capacity = min(token_count, average + average // 2)
    entry_count = token_count * top_count
    flat_ids = expert_ids.reshape(entry_count)
    expert_range = jnp.arange(expert_count, dtype=jnp.int32)
    entry_hot = (expert_ids[:, :, None] == expert_range[None, None, :]).astype(jnp.float32)
    token_hot = jnp.sum(entry_hot, 1).astype(jnp.bfloat16)
    token_range = jnp.arange(token_count, dtype=jnp.int32)
    lower = (token_range[:, None] > token_range[None, :]).astype(jnp.bfloat16)
    before = jnp.dot(lower, token_hot, preferred_element_type=jnp.float32)
    earlier = jnp.sum(before[:, None, :] * entry_hot, 2).reshape(entry_count).astype(jnp.int32)
    position = flat_ids * capacity + earlier
    slot_entry = (
        jnp.full((expert_count * capacity,), entry_count, jnp.int32)
        .at[position]
        .set(jnp.arange(entry_count, dtype=jnp.int32))
    )
    slot_token = slot_entry // top_count
    gate_flat = jnp.concatenate([gates.reshape(entry_count), jnp.zeros((1,), jnp.float32)])
    slot_gate = gate_flat[slot_entry]
    x_source = lax.all_gather(tokens, "half", axis=1, tiled=True)
    dy_source = lax.all_gather(grad_out, "half", axis=1, tiled=True)
    x_send = padded_rows(x_source, slot_token)
    grad_send = (
        slot_gate[:, None] * padded_rows(dy_source, slot_token).astype(jnp.float32)
    ).astype(jnp.bfloat16)
    block_shape = (expert_count, capacity, x_send.shape[1])
    x_recv, grad_recv = dispatch_rows(x_send.reshape(block_shape), grad_send.reshape(block_shape))
    width = x_recv.shape[2]
    own_width = width // half_count
    row_total = expert_count * capacity
    x_rows = x_recv.reshape(row_total, width)
    grad_rows = grad_recv.reshape(row_total, width)
    gate_mat = w_gate[0]
    up_mat = w_up[0]
    down_mat = w_down[0]
    pre_gate = jnp.dot(x_rows, gate_mat, preferred_element_type=jnp.float32)
    pre_up = jnp.dot(x_rows, up_mat, preferred_element_type=jnp.float32)
    sigmoid_gate = jax.nn.sigmoid(pre_gate)
    act = (pre_gate * sigmoid_gate * pre_up).astype(jnp.bfloat16)
    partial_out = jnp.dot(act, down_mat, preferred_element_type=jnp.float32).astype(jnp.bfloat16)
    out_back = return_outputs(partial_out.reshape(expert_count, capacity, width))
    contract_last = (((1,), (1,)), ((), ()))
    contract_rows = (((0,), (0,)), ((), ()))
    grad_act = lax.dot_general(
        grad_rows, down_mat, contract_last, preferred_element_type=jnp.float32
    )
    grad_pre_gate = (
        grad_act * pre_up * sigmoid_gate * (1.0 + pre_gate * (1.0 - sigmoid_gate))
    ).astype(jnp.bfloat16)
    grad_pre_up = (grad_act * pre_gate * sigmoid_gate).astype(jnp.bfloat16)
    partial_grad = lax.dot_general(
        grad_pre_gate, gate_mat, contract_last, preferred_element_type=jnp.float32
    )
    partial_grad = (
        partial_grad
        + lax.dot_general(grad_pre_up, up_mat, contract_last, preferred_element_type=jnp.float32)
    ).astype(jnp.bfloat16)
    grad_back = return_grads(partial_grad.reshape(expert_count, capacity, width))
    grad_gate_mat = lax.dot_general(
        x_rows, grad_pre_gate, contract_rows, preferred_element_type=jnp.float32
    )
    grad_up_mat = lax.dot_general(
        x_rows, grad_pre_up, contract_rows, preferred_element_type=jnp.float32
    )
    grad_down_mat = lax.dot_general(
        act, grad_rows, contract_rows, preferred_element_type=jnp.float32
    )
    back_width = out_back.shape[2]
    routed_out = out_back.reshape(row_total, back_width)[position]
    routed_grad = grad_back.reshape(row_total, back_width)[position]
    split_shape = (entry_count, half_count, own_width)
    moved_out, moved_grad = (
        lax.all_to_all(
            routed_out.reshape(split_shape), "half", split_axis=1, concat_axis=1, tiled=True
        ),
        lax.all_to_all(
            routed_grad.reshape(split_shape), "half", split_axis=1, concat_axis=1, tiled=True
        ),
    )
    expert_out = partner_total(moved_out)
    expert_grad = partner_total(moved_grad)
    expert_out = expert_out.reshape(token_count, top_count, own_width).astype(jnp.float32)
    expert_grad = expert_grad.reshape(token_count, top_count, own_width).astype(jnp.float32)
    mixed = jnp.sum(gates[:, :, None] * expert_out, 1).astype(jnp.bfloat16)
    gate_terms = jnp.sum(grad_out.astype(jnp.float32)[:, None, :] * expert_out, 2)
    grad_gates = lax.psum(gate_terms, "half")
    grad_tokens = jnp.sum(expert_grad, 1).astype(jnp.bfloat16)
    return (
        mixed,
        grad_tokens,
        grad_gates,
        grad_gate_mat.astype(jnp.bfloat16)[None],
        grad_up_mat.astype(jnp.bfloat16)[None],
        grad_down_mat.astype(jnp.bfloat16)[None],
    )


META = 16
LEADING = (((0,), (0,)), ((), ()))
TRAILING = (((1,), (1,)), ((), ()))
CHIPS = 4
COST = {'join': 1.0, 'pack': 0, 'expert': 0, 'merge': 150, 'weight': 0}
WHEN = 0
CHAINZ = 0
FAR = 0
WPOS = 2
BEHIND = 1
STRICT = 0
AHEAD = 1
WEIGHT_A = 1
WEIGHT_B = 2
VMEM = pl.BlockSpec(memory_space=pltpu.VMEM)
SMEM = pl.BlockSpec(memory_space=pltpu.SMEM)


def plane_fits(mesh):
    size = mesh.shape
    return size["groups"] == 1 and size["half"] == 1 and size["col"] == 4 and size["row"] % 2 == 0 and size["row"] <= 32


def dot(left, right, dims=(((1,), (0,)), ((), ()))):
    return lax.dot_general(left, right, dims, preferred_element_type=jnp.float32)


def call(kernel, name, outs, in_specs, flops=0, moved=0, grid=()):
    used = len(in_specs)

    def ordered(*refs):
        kernel(*refs[:used], *refs[used + 1 :])

    return pl.pallas_call(
        ordered,
        out_shape=outs,
        grid=grid,
        in_specs=in_specs + [pl.BlockSpec(memory_space=pl.ANY)],
        out_specs=[VMEM] * len(outs),
        compiler_params=pltpu.CompilerParams(vmem_limit_bytes=56 * 1024 * 1024),
        cost_estimate=pl.CostEstimate(flops=int(flops * COST[name]), bytes_accessed=moved if COST[name] > 0.5 else 0, transcendentals=0),
        name=name,
    )


def split_parts(value):
    first = value.astype(jnp.bfloat16)
    rest = value - first.astype(jnp.float32)
    second = rest.astype(jnp.bfloat16)
    third = (rest - second.astype(jnp.float32)).astype(jnp.bfloat16)
    return first, second, third


def store_meta(ref, pieces):
    tokens = pieces[0].shape[1]
    base = ref.shape[0] - META
    ref[base:, :] = jnp.zeros((META, ref.shape[1]), jnp.bfloat16)
    for number, piece in enumerate(pieces):
        piece = piece.astype(jnp.float32)
        missing = META - piece.shape[0]
        if missing:
            piece = jnp.concatenate([piece, jnp.zeros((missing, tokens), jnp.float32)], 0)
        ref[base:, number * tokens : (number + 1) * tokens] = piece.astype(jnp.bfloat16)


def load_meta(ref, tokens, number):
    base = ref.shape[0] - META
    return ref[base:, number * tokens : (number + 1) * tokens].astype(jnp.float32)


def join_kernel(tokens_ref, grad_ref, ids_ref, gates_ref, block_ref):
    tokens = tokens_ref.shape[0]
    block_ref[:tokens, :] = tokens_ref[...]
    block_ref[tokens : 2 * tokens, :] = grad_ref[...]
    store_meta(block_ref, (ids_ref[...].astype(jnp.float32).astype(jnp.bfloat16),) + split_parts(gates_ref[...]))


def selection(table_ref, block_ref, tokens, capacity, top):
    ids = load_meta(block_ref, tokens, 0)
    gates = load_meta(block_ref, tokens, 1) + load_meta(block_ref, tokens, 2) + load_meta(block_ref, tokens, 3)
    experts = [table_ref[place].astype(jnp.float32) for place in range(2 * CHIPS)]
    live = lax.broadcasted_iota(jnp.int32, ids.shape, 0) < top
    named = [(ids == expert) & live for expert in experts]
    hits = jnp.concatenate([jnp.sum(jnp.where(hit, 1.0, 0.0), 0, keepdims=True) for hit in named], 0)
    weights = [jnp.sum(jnp.where(hit, gates, 0.0), 0, keepdims=True) for hit in named]
    row = lax.broadcasted_iota(jnp.int32, (tokens, tokens), 0)
    column = lax.broadcasted_iota(jnp.int32, (tokens, tokens), 1)
    earlier = dot(hits.astype(jnp.bfloat16), jnp.where(row < column, 1.0, 0.0).astype(jnp.bfloat16))
    slot = lax.broadcasted_iota(jnp.int32, (capacity, tokens), 0).astype(jnp.float32)
    chosen = [
        jnp.where((slot == earlier[place : place + 1]) & (hits[place : place + 1] > 0.0), 1.0, 0.0)
        for place in range(2 * CHIPS)
    ]
    return chosen, weights, named


def pack_kernel(tokens, capacity, top, table_ref, block_ref, *out_refs):
    chosen, weights, _ = selection(table_ref, block_ref, tokens, capacity, top)
    stacked = jnp.concatenate(chosen, 0).astype(jnp.bfloat16)
    slot_gate = jnp.concatenate(
        [jnp.sum(pick * weight, 1, keepdims=True) for pick, weight in zip(chosen, weights)], 0
    )
    rows = dot(stacked, block_ref[:tokens, :]).astype(jnp.bfloat16)
    grads = (slot_gate * dot(stacked, block_ref[tokens : 2 * tokens, :])).astype(jnp.bfloat16)
    for place in range(2 * CHIPS):
        part = slice(place * capacity, (place + 1) * capacity)
        out_refs[place // 2][place % 2, :capacity, :] = rows[part]
        out_refs[place // 2][place % 2, capacity:, :] = grads[part]


def expert_kernel(capacity, *refs):
    in_refs, weight_refs, out_refs = refs[:CHIPS], refs[CHIPS : CHIPS + 6], refs[CHIPS + 6 : 2 * CHIPS + 6]
    rows_ref, grads_ref, act_ref, pre_gate_ref, pre_up_ref = refs[2 * CHIPS + 6 :]
    for core in range(2):
        gate_ref, up_ref, down_ref = weight_refs[3 * core : 3 * core + 3]
        rows = jnp.concatenate([ref[core, :capacity] for ref in in_refs], 0)
        grads = jnp.concatenate([ref[core, capacity:] for ref in in_refs], 0)
        rows_ref[core] = rows
        grads_ref[core] = grads
        pre_gate = dot(rows, gate_ref[...])
        pre_up = dot(rows, up_ref[...])
        sigmoid_gate = jax.nn.sigmoid(pre_gate)
        act = (pre_gate * sigmoid_gate * pre_up).astype(jnp.bfloat16)
        act_ref[core] = act
        out = dot(act, down_ref[...]).astype(jnp.bfloat16)
        grad_act = dot(grads, down_ref[...], TRAILING)
        grad_pre_gate = (
            grad_act * pre_up * sigmoid_gate * (1.0 + pre_gate * (1.0 - sigmoid_gate))
        ).astype(jnp.bfloat16)
        grad_pre_up = (grad_act * pre_gate * sigmoid_gate).astype(jnp.bfloat16)
        pre_gate_ref[core] = grad_pre_gate
        pre_up_ref[core] = grad_pre_up
        grad_in = (
            dot(grad_pre_gate, gate_ref[...], TRAILING) + dot(grad_pre_up, up_ref[...], TRAILING)
        ).astype(jnp.bfloat16)
        for chip in range(CHIPS):
            part = slice(chip * capacity, (chip + 1) * capacity)
            out_refs[chip][core, :capacity, :] = out[part]
            out_refs[chip][core, capacity:, :] = grad_in[part]


def merge_kernel(tokens, capacity, top, before, table_ref, block_ref, *refs):
    back_refs, earlier_refs, out_refs = refs[:CHIPS], refs[CHIPS : CHIPS + before], refs[CHIPS + before :]
    chosen, weights, named = selection(table_ref, block_ref, tokens, capacity, top)
    pieces = [ref[core] for ref in back_refs for core in range(2)]
    out = jnp.concatenate([piece[:capacity] for piece in pieces], 0)
    grad = jnp.concatenate([piece[capacity:] for piece in pieces], 0)
    stacked = jnp.concatenate(chosen, 0).astype(jnp.bfloat16)
    weighted = jnp.concatenate([pick * weight for pick, weight in zip(chosen, weights)], 0)
    high, low, _ = split_parts(weighted)
    mixed = dot(high, out, LEADING) + dot(low, out, LEADING)
    grad_in = dot(stacked, grad, LEADING)
    source = dot(stacked, block_ref[tokens : 2 * tokens, :])
    terms = jnp.sum(source * out.astype(jnp.float32), 1, keepdims=True)
    total = jnp.zeros(named[0].shape, jnp.float32)
    for place in range(2 * CHIPS):
        part = slice(place * capacity, (place + 1) * capacity)
        per_token = jnp.sum(chosen[place] * terms[part], 0, keepdims=True)
        total = total + jnp.where(named[place], per_token, 0.0)
    for ref in earlier_refs:
        mixed = mixed + ref[:tokens, :].astype(jnp.float32)
        grad_in = grad_in + ref[tokens : 2 * tokens, :].astype(jnp.float32)
        total = total + sum(load_meta(ref, tokens, number) for number in range(3))
    if len(out_refs) == 1:
        out_refs[0][:tokens, :] = mixed.astype(jnp.bfloat16)
        out_refs[0][tokens : 2 * tokens, :] = grad_in.astype(jnp.bfloat16)
        store_meta(out_refs[0], split_parts(total))
    else:
        out_refs[0][...] = mixed.astype(jnp.bfloat16)
        out_refs[1][...] = grad_in.astype(jnp.bfloat16)
        out_refs[2][...] = total[:top]


def weight_kernel(levels, *refs):
    steps = [refs[number : number + 5] for number in range(0, 5 * levels, 5)]
    gate_mat = sum(dot(rows[0], gate[0], LEADING) for rows, _, _, gate, _ in steps)
    up_mat = sum(dot(rows[0], up[0], LEADING) for rows, _, _, _, up in steps)
    down_mat = sum(dot(act[0], grads[0], LEADING) for _, grads, act, _, _ in steps)
    width, hidden = gate_mat.shape
    if len(refs) == 5 * levels + 1:
        refs[-1][:width, :hidden] = gate_mat.astype(jnp.bfloat16)
        refs[-1][:width, hidden:] = up_mat.astype(jnp.bfloat16)
        refs[-1][width:, :] = down_mat.astype(jnp.bfloat16)
        return
    other_ref, (gate_ref, up_ref, down_ref) = refs[5 * levels], refs[-3:]
    gate_ref[...] = (gate_mat + other_ref[:width, :hidden].astype(jnp.float32)).astype(jnp.bfloat16)
    up_ref[...] = (up_mat + other_ref[:width, hidden:].astype(jnp.float32)).astype(jnp.bfloat16)
    down_ref[...] = (down_mat + other_ref[width:, :].astype(jnp.float32)).astype(jnp.bfloat16)


def local_plane(tokens, expert_ids, gates, w_gate, w_up, w_down, grad_out):
    token_count, top_count = expert_ids.shape
    width = tokens.shape[1]
    hidden = w_gate.shape[2]
    axes = ("row", "col")
    plane = 2 * CHIPS
    device_count = lax.axis_size("row") * lax.axis_size("col")
    levels = device_count // plane
    average = token_count * top_count // device_count
    capacity = -(-min(token_count, average + average // 2) // 16) * 16
    me = lax.axis_index("row") * lax.axis_size("col") + lax.axis_index("col")
    table = (me // plane) * plane + jnp.bitwise_xor(me % plane, jnp.arange(plane, dtype=jnp.int32))
    bf16 = functools.partial(jax.ShapeDtypeStruct, dtype=jnp.bfloat16)

    def flip(value, mask):
        pairs = [(device, device ^ mask) for device in range(device_count)]
        return lax.ppermute(value, axes, pairs)

    def climb(value, step):
        pairs = [(device, (device + step * plane) % device_count) for device in range(device_count)]
        return lax.ppermute(value, axes, pairs)

    block_rows = 2 * token_count + META
    row_total = plane * capacity
    pair = bf16((2, 2 * capacity, width))
    half_rows = row_total // 2
    (block,) = call(join_kernel, "join", [bf16((block_rows, width))], [VMEM] * 4, 0, 4 * block_rows * width)(
        tokens, grad_out, expert_ids.T, gates.T, gates
    )
    order = sorted(range(levels), key=lambda step: min(step, levels - step))
    pack = call(
        functools.partial(pack_kernel, token_count, capacity, top_count),
        "pack",
        [pair] * CHIPS,
        [SMEM, VMEM],
        4 * row_total * token_count * width,
        2 * (block_rows + 2 * row_total) * width,
    )
    kept_shapes = [bf16((2, half_rows, size)) for size in (width, width, hidden, hidden, hidden)]
    expert = call(
        functools.partial(expert_kernel, capacity),
        "expert",
        [pair] * CHIPS + kept_shapes,
        [VMEM] * (CHIPS + 6),
        12 * row_total * width * hidden,
        2 * (6 * row_total * width + 3 * row_total * hidden + 6 * width * hidden),
    )
    half_block = bf16((token_count, width))
    results_shapes = [half_block, half_block, jax.ShapeDtypeStruct((top_count, token_count), jnp.float32)]

    def merge(before, final):
        return call(
            functools.partial(merge_kernel, token_count, capacity, top_count, before),
            "merge",
            results_shapes if final else [bf16((block_rows, width))],
            [SMEM] + [VMEM] * (1 + CHIPS + before),
            8 * row_total * token_count * width,
            2 * (2 * block_rows + 2 * row_total) * width,
        )

    def weight(core, partials):
        specs = [
            pl.BlockSpec((1,) + shape.shape[1:], lambda step: (core, 0, 0), memory_space=pltpu.VMEM) for shape in kept_shapes
        ]
        return call(
            functools.partial(weight_kernel, levels),
            "weight",
            [bf16((width, hidden)), bf16((width, hidden)), bf16((hidden, width))]
            if partials
            else [bf16((width + hidden, 2 * hidden))],
            specs * levels + [VMEM] * partials,
            3 * levels * row_total * width * hidden,
            levels * row_total * (2 * width + 3 * hidden) + 6 * width * hidden,
            (1,),
        )

    def after(value, *earlier):
        return lax.optimization_barrier((value,) + earlier)[0]

    moved = []

    def exchange(parts):
        earlier = moved[-BEHIND] if len(moved) >= BEHIND else None
        received = [parts[0]]
        for chip in range(1, CHIPS):
            part = after(parts[chip], *(earlier[1:] if STRICT else earlier[chip : chip + 1])) if earlier else parts[chip]
            received.append(flip(part, 2 * chip))
        moved.append(received)
        return received

    mats = [w_gate[0], w_up[0], w_down[0]]
    blocks = {0: block}
    for step in order[1:]:
        blocks[step] = climb(after(block, blocks[order[1]]) if CHAINZ and step == order[-2] else block, step)
    arrived, results, kept = {}, {}, {}
    last = block
    for turn in range(levels + AHEAD):
        if turn == min(WHEN, levels - 1):
            for mat in mats[:3]:
                mats.append(flip(mat, 1))
            last = after(last, *mats[3:])
        if turn < levels:
            packed = pack(table, blocks[order[turn]], last)
            last = packed[0]
            arrived[order[turn]] = exchange(packed)
        if turn >= AHEAD:
            step = order[turn - AHEAD]
            outs = expert(*arrived[step], *mats, last)
            last = outs[0]
            results[step], kept[step] = outs[:CHIPS], outs[CHIPS:]
    homeward = (sorted(order[1:], key=lambda step: -min(step, levels - step)) if FAR else order[1:]) + order[:1]
    returned = {step: exchange(results[step]) for step in homeward}
    saved = [value for step in order for value in kept[step]]
    sent = []
    for turn, step in enumerate(homeward):
        if turn == WPOS:
            (partial,) = weight(1, 0)(*saved, last)
            last = partial
            partial = flip(partial, 1)
        if turn == levels - 1:
            grad_mats = weight(0, 1)(*saved, partial, last)
            last = grad_mats[0]
        earlier, final = (sent, True) if step == 0 else ([], False)
        merged = merge(len(earlier), final)(table, blocks[step], *returned[step], *earlier, last)
        last = merged[0]
        if step:
            sent.append(climb(merged[0], levels - step))
    mixed, grad_tokens, grad_gates = merged
    return (mixed, grad_tokens, grad_gates.T) + tuple(mat[None] for mat in grad_mats)


def solution(mesh):
    return jax.shard_map(
        local_plane if plane_fits(mesh) else local_exchange,
        mesh=mesh,
        in_specs=(
            P(("groups", "row", "col"), "half"),
            P(("groups", "row", "col"), None),
            P(("groups", "row", "col"), None),
            P(("row", "col"), None, "half"),
            P(("row", "col"), None, "half"),
            P(("row", "col"), "half", None),
            P(("groups", "row", "col"), "half"),
        ),
        out_specs=(
            P(("groups", "row", "col"), "half"),
            P(("groups", "row", "col"), "half"),
            P(("groups", "row", "col"), None),
            P(("groups", "row", "col"), None, "half"),
            P(("groups", "row", "col"), None, "half"),
            P(("groups", "row", "col"), "half", None),
        ),
        check_vma=False,
    )
```

```python
import functools

import jax
import jax.numpy as jnp
from jax import lax
from jax.experimental import pallas as pl
from jax.experimental.pallas import tpu as pltpu
from jax.sharding import PartitionSpec as P


def padded_rows(source, slot_token):
    extended = jnp.concatenate([source, jnp.zeros((1, source.shape[1]), source.dtype)])
    return extended[slot_token]


def dispatch_rows(x_block, grad_block):
    return (
        lax.all_to_all(x_block, ("row", "col"), split_axis=0, concat_axis=0, tiled=True),
        lax.all_to_all(grad_block, ("row", "col"), split_axis=0, concat_axis=0, tiled=True),
    )


def return_outputs(block):
    return lax.all_to_all(block, ("row", "col"), split_axis=0, concat_axis=0, tiled=True)


def return_grads(block):
    return lax.all_to_all(block, ("row", "col"), split_axis=0, concat_axis=0, tiled=True)


def partner_total(moved):
    return jnp.sum(moved.astype(jnp.float32), 1).astype(jnp.bfloat16)


def local_exchange(tokens, expert_ids, gates, w_gate, w_up, w_down, grad_out):
    token_count, top_count = expert_ids.shape
    expert_count = lax.axis_size("row") * lax.axis_size("col")
    half_count = lax.axis_size("half")
    average = token_count * top_count // expert_count
    capacity = min(token_count, average + average // 2)
    entry_count = token_count * top_count
    flat_ids = expert_ids.reshape(entry_count)
    expert_range = jnp.arange(expert_count, dtype=jnp.int32)
    entry_hot = (expert_ids[:, :, None] == expert_range[None, None, :]).astype(jnp.float32)
    token_hot = jnp.sum(entry_hot, 1).astype(jnp.bfloat16)
    token_range = jnp.arange(token_count, dtype=jnp.int32)
    lower = (token_range[:, None] > token_range[None, :]).astype(jnp.bfloat16)
    before = jnp.dot(lower, token_hot, preferred_element_type=jnp.float32)
    earlier = jnp.sum(before[:, None, :] * entry_hot, 2).reshape(entry_count).astype(jnp.int32)
    position = flat_ids * capacity + earlier
    slot_entry = (
        jnp.full((expert_count * capacity,), entry_count, jnp.int32)
        .at[position]
        .set(jnp.arange(entry_count, dtype=jnp.int32))
    )
    slot_token = slot_entry // top_count
    gate_flat = jnp.concatenate([gates.reshape(entry_count), jnp.zeros((1,), jnp.float32)])
    slot_gate = gate_flat[slot_entry]
    x_source = lax.all_gather(tokens, "half", axis=1, tiled=True)
    dy_source = lax.all_gather(grad_out, "half", axis=1, tiled=True)
    x_send = padded_rows(x_source, slot_token)
    grad_send = (
        slot_gate[:, None] * padded_rows(dy_source, slot_token).astype(jnp.float32)
    ).astype(jnp.bfloat16)
    block_shape = (expert_count, capacity, x_send.shape[1])
    x_recv, grad_recv = dispatch_rows(x_send.reshape(block_shape), grad_send.reshape(block_shape))
    width = x_recv.shape[2]
    own_width = width // half_count
    row_total = expert_count * capacity
    x_rows = x_recv.reshape(row_total, width)
    grad_rows = grad_recv.reshape(row_total, width)
    gate_mat = w_gate[0]
    up_mat = w_up[0]
    down_mat = w_down[0]
    pre_gate = jnp.dot(x_rows, gate_mat, preferred_element_type=jnp.float32)
    pre_up = jnp.dot(x_rows, up_mat, preferred_element_type=jnp.float32)
    sigmoid_gate = jax.nn.sigmoid(pre_gate)
    act = (pre_gate * sigmoid_gate * pre_up).astype(jnp.bfloat16)
    partial_out = jnp.dot(act, down_mat, preferred_element_type=jnp.float32).astype(jnp.bfloat16)
    out_back = return_outputs(partial_out.reshape(expert_count, capacity, width))
    contract_last = (((1,), (1,)), ((), ()))
    contract_rows = (((0,), (0,)), ((), ()))
    grad_act = lax.dot_general(
        grad_rows, down_mat, contract_last, preferred_element_type=jnp.float32
    )
    grad_pre_gate = (
        grad_act * pre_up * sigmoid_gate * (1.0 + pre_gate * (1.0 - sigmoid_gate))
    ).astype(jnp.bfloat16)
    grad_pre_up = (grad_act * pre_gate * sigmoid_gate).astype(jnp.bfloat16)
    partial_grad = lax.dot_general(
        grad_pre_gate, gate_mat, contract_last, preferred_element_type=jnp.float32
    )
    partial_grad = (
        partial_grad
        + lax.dot_general(grad_pre_up, up_mat, contract_last, preferred_element_type=jnp.float32)
    ).astype(jnp.bfloat16)
    grad_back = return_grads(partial_grad.reshape(expert_count, capacity, width))
    grad_gate_mat = lax.dot_general(
        x_rows, grad_pre_gate, contract_rows, preferred_element_type=jnp.float32
    )
    grad_up_mat = lax.dot_general(
        x_rows, grad_pre_up, contract_rows, preferred_element_type=jnp.float32
    )
    grad_down_mat = lax.dot_general(
        act, grad_rows, contract_rows, preferred_element_type=jnp.float32
    )
    back_width = out_back.shape[2]
    routed_out = out_back.reshape(row_total, back_width)[position]
    routed_grad = grad_back.reshape(row_total, back_width)[position]
    split_shape = (entry_count, half_count, own_width)
    moved_out, moved_grad = (
        lax.all_to_all(
            routed_out.reshape(split_shape), "half", split_axis=1, concat_axis=1, tiled=True
        ),
        lax.all_to_all(
            routed_grad.reshape(split_shape), "half", split_axis=1, concat_axis=1, tiled=True
        ),
    )
    expert_out = partner_total(moved_out)
    expert_grad = partner_total(moved_grad)
    expert_out = expert_out.reshape(token_count, top_count, own_width).astype(jnp.float32)
    expert_grad = expert_grad.reshape(token_count, top_count, own_width).astype(jnp.float32)
    mixed = jnp.sum(gates[:, :, None] * expert_out, 1).astype(jnp.bfloat16)
    gate_terms = jnp.sum(grad_out.astype(jnp.float32)[:, None, :] * expert_out, 2)
    grad_gates = lax.psum(gate_terms, "half")
    grad_tokens = jnp.sum(expert_grad, 1).astype(jnp.bfloat16)
    return (
        mixed,
        grad_tokens,
        grad_gates,
        grad_gate_mat.astype(jnp.bfloat16)[None],
        grad_up_mat.astype(jnp.bfloat16)[None],
        grad_down_mat.astype(jnp.bfloat16)[None],
    )


META = 16
LEADING = (((0,), (0,)), ((), ()))
TRAILING = (((1,), (1,)), ((), ()))
CHIPS = 4
COST = {'join': 1.0, 'pack': 0, 'expert': 0, 'merge': 150, 'weight': 0}
WHEN = 0
CHAINZ = 0
WPOS = 2
BEHIND = 1
STRICT = 0
AHEAD = 1
VMEM = pl.BlockSpec(memory_space=pltpu.VMEM)
SMEM = pl.BlockSpec(memory_space=pltpu.SMEM)


def plane_fits(mesh):
    size = mesh.shape
    return size["groups"] == 1 and size["half"] == 1 and size["col"] == 4 and size["row"] % 2 == 0 and size["row"] <= 32


def dot(left, right, dims=(((1,), (0,)), ((), ()))):
    return lax.dot_general(left, right, dims, preferred_element_type=jnp.float32)


def call(kernel, name, outs, in_specs, flops=0, moved=0, grid=()):
    used = len(in_specs)

    def ordered(*refs):
        kernel(*refs[:used], *refs[used + 1 :])

    return pl.pallas_call(
        ordered,
        out_shape=outs,
        grid=grid,
        in_specs=in_specs + [pl.BlockSpec(memory_space=pl.ANY)],
        out_specs=[VMEM] * len(outs),
        compiler_params=pltpu.CompilerParams(vmem_limit_bytes=56 * 1024 * 1024),
        cost_estimate=pl.CostEstimate(flops=int(flops * COST[name]), bytes_accessed=moved if COST[name] > 0.5 else 0, transcendentals=0),
        name=name,
    )


def split_parts(value):
    first = value.astype(jnp.bfloat16)
    rest = value - first.astype(jnp.float32)
    second = rest.astype(jnp.bfloat16)
    third = (rest - second.astype(jnp.float32)).astype(jnp.bfloat16)
    return first, second, third


def store_meta(ref, pieces):
    tokens = pieces[0].shape[1]
    base = ref.shape[0] - META
    ref[base:, :] = jnp.zeros((META, ref.shape[1]), jnp.bfloat16)
    for number, piece in enumerate(pieces):
        piece = piece.astype(jnp.float32)
        missing = META - piece.shape[0]
        if missing:
            piece = jnp.concatenate([piece, jnp.zeros((missing, tokens), jnp.float32)], 0)
        ref[base:, number * tokens : (number + 1) * tokens] = piece.astype(jnp.bfloat16)


def load_meta(ref, tokens, number):
    base = ref.shape[0] - META
    return ref[base:, number * tokens : (number + 1) * tokens].astype(jnp.float32)


def join_kernel(tokens_ref, grad_ref, ids_ref, gates_ref, block_ref):
    tokens = tokens_ref.shape[0]
    block_ref[:tokens, :] = tokens_ref[...]
    block_ref[tokens : 2 * tokens, :] = grad_ref[...]
    store_meta(block_ref, (ids_ref[...].astype(jnp.float32).astype(jnp.bfloat16),) + split_parts(gates_ref[...]))


def selection(table_ref, block_ref, tokens, capacity, top):
    ids = load_meta(block_ref, tokens, 0)
    gates = load_meta(block_ref, tokens, 1) + load_meta(block_ref, tokens, 2) + load_meta(block_ref, tokens, 3)
    experts = [table_ref[place].astype(jnp.float32) for place in range(2 * CHIPS)]
    live = lax.broadcasted_iota(jnp.int32, ids.shape, 0) < top
    named = [(ids == expert) & live for expert in experts]
    hits = jnp.concatenate([jnp.sum(jnp.where(hit, 1.0, 0.0), 0, keepdims=True) for hit in named], 0)
    weights = [jnp.sum(jnp.where(hit, gates, 0.0), 0, keepdims=True) for hit in named]
    row = lax.broadcasted_iota(jnp.int32, (tokens, tokens), 0)
    column = lax.broadcasted_iota(jnp.int32, (tokens, tokens), 1)
    earlier = dot(hits.astype(jnp.bfloat16), jnp.where(row < column, 1.0, 0.0).astype(jnp.bfloat16))
    slot = lax.broadcasted_iota(jnp.int32, (capacity, tokens), 0).astype(jnp.float32)
    chosen = [
        jnp.where((slot == earlier[place : place + 1]) & (hits[place : place + 1] > 0.0), 1.0, 0.0)
        for place in range(2 * CHIPS)
    ]
    return chosen, weights, named


def pack_kernel(tokens, capacity, top, table_ref, block_ref, *out_refs):
    chosen, weights, _ = selection(table_ref, block_ref, tokens, capacity, top)
    stacked = jnp.concatenate(chosen, 0).astype(jnp.bfloat16)
    slot_gate = jnp.concatenate(
        [jnp.sum(pick * weight, 1, keepdims=True) for pick, weight in zip(chosen, weights)], 0
    )
    rows = dot(stacked, block_ref[:tokens, :]).astype(jnp.bfloat16)
    grads = (slot_gate * dot(stacked, block_ref[tokens : 2 * tokens, :])).astype(jnp.bfloat16)
    for place in range(2 * CHIPS):
        part = slice(place * capacity, (place + 1) * capacity)
        out_refs[place // 2][place % 2, :capacity, :] = rows[part]
        out_refs[place // 2][place % 2, capacity:, :] = grads[part]


def expert_kernel(capacity, *refs):
    in_refs, weight_refs, out_refs = refs[:CHIPS], refs[CHIPS : CHIPS + 6], refs[CHIPS + 6 : 2 * CHIPS + 6]
    rows_ref, grads_ref, act_ref, pre_gate_ref, pre_up_ref = refs[2 * CHIPS + 6 :]
    for core in range(2):
        gate_ref, up_ref, down_ref = weight_refs[3 * core : 3 * core + 3]
        rows = jnp.concatenate([ref[core, :capacity] for ref in in_refs], 0)
        grads = jnp.concatenate([ref[core, capacity:] for ref in in_refs], 0)
        rows_ref[core] = rows
        grads_ref[core] = grads
        pre_gate = dot(rows, gate_ref[...])
        pre_up = dot(rows, up_ref[...])
        sigmoid_gate = jax.nn.sigmoid(pre_gate)
        act = (pre_gate * sigmoid_gate * pre_up).astype(jnp.bfloat16)
        act_ref[core] = act
        out = dot(act, down_ref[...]).astype(jnp.bfloat16)
        grad_act = dot(grads, down_ref[...], TRAILING)
        grad_pre_gate = (
            grad_act * pre_up * sigmoid_gate * (1.0 + pre_gate * (1.0 - sigmoid_gate))
        ).astype(jnp.bfloat16)
        grad_pre_up = (grad_act * pre_gate * sigmoid_gate).astype(jnp.bfloat16)
        pre_gate_ref[core] = grad_pre_gate
        pre_up_ref[core] = grad_pre_up
        grad_in = (
            dot(grad_pre_gate, gate_ref[...], TRAILING) + dot(grad_pre_up, up_ref[...], TRAILING)
        ).astype(jnp.bfloat16)
        for chip in range(CHIPS):
            part = slice(chip * capacity, (chip + 1) * capacity)
            out_refs[chip][core, :capacity, :] = out[part]
            out_refs[chip][core, capacity:, :] = grad_in[part]


def merge_kernel(tokens, capacity, top, before, table_ref, block_ref, *refs):
    back_refs, earlier_refs, out_refs = refs[:CHIPS], refs[CHIPS : CHIPS + before], refs[CHIPS + before :]
    chosen, weights, named = selection(table_ref, block_ref, tokens, capacity, top)
    pieces = [ref[core] for ref in back_refs for core in range(2)]
    out = jnp.concatenate([piece[:capacity] for piece in pieces], 0)
    grad = jnp.concatenate([piece[capacity:] for piece in pieces], 0)
    stacked = jnp.concatenate(chosen, 0).astype(jnp.bfloat16)
    weighted = jnp.concatenate([pick * weight for pick, weight in zip(chosen, weights)], 0)
    high, low, _ = split_parts(weighted)
    mixed = dot(high, out, LEADING) + dot(low, out, LEADING)
    grad_in = dot(stacked, grad, LEADING)
    source = dot(stacked, block_ref[tokens : 2 * tokens, :])
    terms = jnp.sum(source * out.astype(jnp.float32), 1, keepdims=True)
    total = jnp.zeros(named[0].shape, jnp.float32)
    for place in range(2 * CHIPS):
        part = slice(place * capacity, (place + 1) * capacity)
        per_token = jnp.sum(chosen[place] * terms[part], 0, keepdims=True)
        total = total + jnp.where(named[place], per_token, 0.0)
    for ref in earlier_refs:
        mixed = mixed + ref[:tokens, :].astype(jnp.float32)
        grad_in = grad_in + ref[tokens : 2 * tokens, :].astype(jnp.float32)
        total = total + sum(load_meta(ref, tokens, number) for number in range(3))
    if len(out_refs) == 1:
        out_refs[0][:tokens, :] = mixed.astype(jnp.bfloat16)
        out_refs[0][tokens : 2 * tokens, :] = grad_in.astype(jnp.bfloat16)
        store_meta(out_refs[0], split_parts(total))
    else:
        out_refs[0][...] = mixed.astype(jnp.bfloat16)
        out_refs[1][...] = grad_in.astype(jnp.bfloat16)
        out_refs[2][...] = total[:top]


def weight_kernel(levels, *refs):
    steps = [refs[number : number + 5] for number in range(0, 5 * levels, 5)]
    gate_mat = sum(dot(rows[0], gate[0], LEADING) for rows, _, _, gate, _ in steps)
    up_mat = sum(dot(rows[0], up[0], LEADING) for rows, _, _, _, up in steps)
    down_mat = sum(dot(act[0], grads[0], LEADING) for _, grads, act, _, _ in steps)
    width, hidden = gate_mat.shape
    if len(refs) == 5 * levels + 1:
        refs[-1][:width, :hidden] = gate_mat.astype(jnp.bfloat16)
        refs[-1][:width, hidden:] = up_mat.astype(jnp.bfloat16)
        refs[-1][width:, :] = down_mat.astype(jnp.bfloat16)
        return
    other_ref, (gate_ref, up_ref, down_ref) = refs[5 * levels], refs[-3:]
    gate_ref[...] = (gate_mat + other_ref[:width, :hidden].astype(jnp.float32)).astype(jnp.bfloat16)
    up_ref[...] = (up_mat + other_ref[:width, hidden:].astype(jnp.float32)).astype(jnp.bfloat16)
    down_ref[...] = (down_mat + other_ref[width:, :].astype(jnp.float32)).astype(jnp.bfloat16)


def local_plane(tokens, expert_ids, gates, w_gate, w_up, w_down, grad_out):
    token_count, top_count = expert_ids.shape
    width = tokens.shape[1]
    hidden = w_gate.shape[2]
    axes = ("row", "col")
    plane = 2 * CHIPS
    device_count = lax.axis_size("row") * lax.axis_size("col")
    levels = device_count // plane
    average = token_count * top_count // device_count
    capacity = -(-min(token_count, average + average // 2) // 16) * 16
    me = lax.axis_index("row") * lax.axis_size("col") + lax.axis_index("col")
    table = (me // plane) * plane + jnp.bitwise_xor(me % plane, jnp.arange(plane, dtype=jnp.int32))
    bf16 = functools.partial(jax.ShapeDtypeStruct, dtype=jnp.bfloat16)

    def flip(value, mask):
        pairs = [(device, device ^ mask) for device in range(device_count)]
        return lax.ppermute(value, axes, pairs)

    def climb(value, step):
        pairs = [(device, (device + step * plane) % device_count) for device in range(device_count)]
        return lax.ppermute(value, axes, pairs)

    block_rows = 2 * token_count + META
    row_total = plane * capacity
    pair = bf16((2, 2 * capacity, width))
    half_rows = row_total // 2
    (block,) = call(join_kernel, "join", [bf16((block_rows, width))], [VMEM] * 4, 0, 4 * block_rows * width)(
        tokens, grad_out, expert_ids.T, gates.T, gates
    )
    order = sorted(range(levels), key=lambda step: min(step, levels - step))
    pack = call(
        functools.partial(pack_kernel, token_count, capacity, top_count),
        "pack",
        [pair] * CHIPS,
        [SMEM, VMEM],
        4 * row_total * token_count * width,
        2 * (block_rows + 2 * row_total) * width,
    )
    kept_shapes = [bf16((2, half_rows, size)) for size in (width, width, hidden, hidden, hidden)]
    expert = call(
        functools.partial(expert_kernel, capacity),
        "expert",
        [pair] * CHIPS + kept_shapes,
        [VMEM] * (CHIPS + 6),
        12 * row_total * width * hidden,
        2 * (6 * row_total * width + 3 * row_total * hidden + 6 * width * hidden),
    )
    half_block = bf16((token_count, width))
    results_shapes = [half_block, half_block, jax.ShapeDtypeStruct((top_count, token_count), jnp.float32)]

    def merge(before, final):
        return call(
            functools.partial(merge_kernel, token_count, capacity, top_count, before),
            "merge",
            results_shapes if final else [bf16((block_rows, width))],
            [SMEM] + [VMEM] * (1 + CHIPS + before),
            8 * row_total * token_count * width,
            2 * (2 * block_rows + 2 * row_total) * width,
        )

    def weight(core, partials):
        specs = [
            pl.BlockSpec((1,) + shape.shape[1:], lambda step: (core, 0, 0), memory_space=pltpu.VMEM) for shape in kept_shapes
        ]
        return call(
            functools.partial(weight_kernel, levels),
            "weight",
            [bf16((width, hidden)), bf16((width, hidden)), bf16((hidden, width))]
            if partials
            else [bf16((width + hidden, 2 * hidden))],
            specs * levels + [VMEM] * partials,
            3 * levels * row_total * width * hidden,
            levels * row_total * (2 * width + 3 * hidden) + 6 * width * hidden,
            (1,),
        )

    def after(value, *earlier):
        return lax.optimization_barrier((value,) + earlier)[0]

    moved = []

    def exchange(parts):
        earlier = moved[-BEHIND] if len(moved) >= BEHIND else None
        received = [parts[0]]
        for chip in range(1, CHIPS):
            part = after(parts[chip], *(earlier[1:] if STRICT else earlier[chip : chip + 1])) if earlier else parts[chip]
            received.append(flip(part, 2 * chip))
        moved.append(received)
        return received

    mats = [w_gate[0], w_up[0], w_down[0]]
    blocks = {0: block}
    for step in order[1:]:
        blocks[step] = climb(after(block, blocks[order[1]]) if CHAINZ and step == order[-2] else block, step)
    arrived, results, kept = {}, {}, {}
    last = block
    for turn in range(levels + AHEAD):
        if turn == min(WHEN, levels - 1):
            for mat in mats[:3]:
                mats.append(flip(mat, 1))
            last = after(last, *mats[3:])
        if turn < levels:
            packed = pack(table, blocks[order[turn]], last)
            last = packed[0]
            arrived[order[turn]] = exchange(packed)
        if turn >= AHEAD:
            step = order[turn - AHEAD]
            outs = expert(*arrived[step], *mats, last)
            last = outs[0]
            results[step], kept[step] = outs[:CHIPS], outs[CHIPS:]
    homeward = order[1:2] + order[:1:-1] + order[:1]
    returned = {step: exchange(results[step]) for step in homeward}
    saved = [value for step in order for value in kept[step]]
    sent = []
    for turn, step in enumerate(homeward):
        if turn == WPOS:
            (partial,) = weight(1, 0)(*saved, last)
            last = partial
            partial = flip(partial, 1)
        if turn == levels - 1:
            grad_mats = weight(0, 1)(*saved, partial, last)
            last = grad_mats[0]
        earlier, final = (sent, True) if step == 0 else ([], False)
        merged = merge(len(earlier), final)(table, blocks[step], *returned[step], *earlier, last)
        last = merged[0]
        if step:
            sent.append(climb(merged[0], levels - step))
    mixed, grad_tokens, grad_gates = merged
    return (mixed, grad_tokens, grad_gates.T) + tuple(mat[None] for mat in grad_mats)


def solution(mesh):
    return jax.shard_map(
        local_plane if plane_fits(mesh) else local_exchange,
        mesh=mesh,
        in_specs=(
            P(("groups", "row", "col"), "half"),
            P(("groups", "row", "col"), None),
            P(("groups", "row", "col"), None),
            P(("row", "col"), None, "half"),
            P(("row", "col"), None, "half"),
            P(("row", "col"), "half", None),
            P(("groups", "row", "col"), "half"),
        ),
        out_specs=(
            P(("groups", "row", "col"), "half"),
            P(("groups", "row", "col"), "half"),
            P(("groups", "row", "col"), None),
            P(("groups", "row", "col"), None, "half"),
            P(("groups", "row", "col"), None, "half"),
            P(("groups", "row", "col"), "half", None),
        ),
        check_vma=False,
    )
```

```python
import functools

import jax
import jax.numpy as jnp
from jax import lax
from jax.experimental import pallas as pl
from jax.experimental.pallas import tpu as pltpu
from jax.sharding import PartitionSpec as P


def padded_rows(source, slot_token):
    extended = jnp.concatenate([source, jnp.zeros((1, source.shape[1]), source.dtype)])
    return extended[slot_token]


def dispatch_rows(x_block, grad_block):
    return (
        lax.all_to_all(x_block, ("row", "col"), split_axis=0, concat_axis=0, tiled=True),
        lax.all_to_all(grad_block, ("row", "col"), split_axis=0, concat_axis=0, tiled=True),
    )


def return_outputs(block):
    return lax.all_to_all(block, ("row", "col"), split_axis=0, concat_axis=0, tiled=True)


def return_grads(block):
    return lax.all_to_all(block, ("row", "col"), split_axis=0, concat_axis=0, tiled=True)


def partner_total(moved):
    return jnp.sum(moved.astype(jnp.float32), 1).astype(jnp.bfloat16)


def local_exchange(tokens, expert_ids, gates, w_gate, w_up, w_down, grad_out):
    token_count, top_count = expert_ids.shape
    expert_count = lax.axis_size("row") * lax.axis_size("col")
    half_count = lax.axis_size("half")
    average = token_count * top_count // expert_count
    capacity = min(token_count, average + average // 2)
    entry_count = token_count * top_count
    flat_ids = expert_ids.reshape(entry_count)
    expert_range = jnp.arange(expert_count, dtype=jnp.int32)
    entry_hot = (expert_ids[:, :, None] == expert_range[None, None, :]).astype(jnp.float32)
    token_hot = jnp.sum(entry_hot, 1).astype(jnp.bfloat16)
    token_range = jnp.arange(token_count, dtype=jnp.int32)
    lower = (token_range[:, None] > token_range[None, :]).astype(jnp.bfloat16)
    before = jnp.dot(lower, token_hot, preferred_element_type=jnp.float32)
    earlier = jnp.sum(before[:, None, :] * entry_hot, 2).reshape(entry_count).astype(jnp.int32)
    position = flat_ids * capacity + earlier
    slot_entry = (
        jnp.full((expert_count * capacity,), entry_count, jnp.int32)
        .at[position]
        .set(jnp.arange(entry_count, dtype=jnp.int32))
    )
    slot_token = slot_entry // top_count
    gate_flat = jnp.concatenate([gates.reshape(entry_count), jnp.zeros((1,), jnp.float32)])
    slot_gate = gate_flat[slot_entry]
    x_source = lax.all_gather(tokens, "half", axis=1, tiled=True)
    dy_source = lax.all_gather(grad_out, "half", axis=1, tiled=True)
    x_send = padded_rows(x_source, slot_token)
    grad_send = (
        slot_gate[:, None] * padded_rows(dy_source, slot_token).astype(jnp.float32)
    ).astype(jnp.bfloat16)
    block_shape = (expert_count, capacity, x_send.shape[1])
    x_recv, grad_recv = dispatch_rows(x_send.reshape(block_shape), grad_send.reshape(block_shape))
    width = x_recv.shape[2]
    own_width = width // half_count
    row_total = expert_count * capacity
    x_rows = x_recv.reshape(row_total, width)
    grad_rows = grad_recv.reshape(row_total, width)
    gate_mat = w_gate[0]
    up_mat = w_up[0]
    down_mat = w_down[0]
    pre_gate = jnp.dot(x_rows, gate_mat, preferred_element_type=jnp.float32)
    pre_up = jnp.dot(x_rows, up_mat, preferred_element_type=jnp.float32)
    sigmoid_gate = jax.nn.sigmoid(pre_gate)
    act = (pre_gate * sigmoid_gate * pre_up).astype(jnp.bfloat16)
    partial_out = jnp.dot(act, down_mat, preferred_element_type=jnp.float32).astype(jnp.bfloat16)
    out_back = return_outputs(partial_out.reshape(expert_count, capacity, width))
    contract_last = (((1,), (1,)), ((), ()))
    contract_rows = (((0,), (0,)), ((), ()))
    grad_act = lax.dot_general(
        grad_rows, down_mat, contract_last, preferred_element_type=jnp.float32
    )
    grad_pre_gate = (
        grad_act * pre_up * sigmoid_gate * (1.0 + pre_gate * (1.0 - sigmoid_gate))
    ).astype(jnp.bfloat16)
    grad_pre_up = (grad_act * pre_gate * sigmoid_gate).astype(jnp.bfloat16)
    partial_grad = lax.dot_general(
        grad_pre_gate, gate_mat, contract_last, preferred_element_type=jnp.float32
    )
    partial_grad = (
        partial_grad
        + lax.dot_general(grad_pre_up, up_mat, contract_last, preferred_element_type=jnp.float32)
    ).astype(jnp.bfloat16)
    grad_back = return_grads(partial_grad.reshape(expert_count, capacity, width))
    grad_gate_mat = lax.dot_general(
        x_rows, grad_pre_gate, contract_rows, preferred_element_type=jnp.float32
    )
    grad_up_mat = lax.dot_general(
        x_rows, grad_pre_up, contract_rows, preferred_element_type=jnp.float32
    )
    grad_down_mat = lax.dot_general(
        act, grad_rows, contract_rows, preferred_element_type=jnp.float32
    )
    back_width = out_back.shape[2]
    routed_out = out_back.reshape(row_total, back_width)[position]
    routed_grad = grad_back.reshape(row_total, back_width)[position]
    split_shape = (entry_count, half_count, own_width)
    moved_out, moved_grad = (
        lax.all_to_all(
            routed_out.reshape(split_shape), "half", split_axis=1, concat_axis=1, tiled=True
        ),
        lax.all_to_all(
            routed_grad.reshape(split_shape), "half", split_axis=1, concat_axis=1, tiled=True
        ),
    )
    expert_out = partner_total(moved_out)
    expert_grad = partner_total(moved_grad)
    expert_out = expert_out.reshape(token_count, top_count, own_width).astype(jnp.float32)
    expert_grad = expert_grad.reshape(token_count, top_count, own_width).astype(jnp.float32)
    mixed = jnp.sum(gates[:, :, None] * expert_out, 1).astype(jnp.bfloat16)
    gate_terms = jnp.sum(grad_out.astype(jnp.float32)[:, None, :] * expert_out, 2)
    grad_gates = lax.psum(gate_terms, "half")
    grad_tokens = jnp.sum(expert_grad, 1).astype(jnp.bfloat16)
    return (
        mixed,
        grad_tokens,
        grad_gates,
        grad_gate_mat.astype(jnp.bfloat16)[None],
        grad_up_mat.astype(jnp.bfloat16)[None],
        grad_down_mat.astype(jnp.bfloat16)[None],
    )


META = 16
LEADING = (((0,), (0,)), ((), ()))
TRAILING = (((1,), (1,)), ((), ()))
CHIPS = 4
COST = {'join': 1.0, 'pack': 0, 'expert': 0, 'merge': 150, 'weight': 25}
WHEN = 0
CHAINZ = 0
WPOS = 2
BEHIND = 1
STRICT = 0
AHEAD = 1
VMEM = pl.BlockSpec(memory_space=pltpu.VMEM)
SMEM = pl.BlockSpec(memory_space=pltpu.SMEM)


def plane_fits(mesh):
    size = mesh.shape
    return size["groups"] == 1 and size["half"] == 1 and size["col"] == 4 and size["row"] % 2 == 0 and size["row"] <= 32


def dot(left, right, dims=(((1,), (0,)), ((), ()))):
    return lax.dot_general(left, right, dims, preferred_element_type=jnp.float32)


def call(kernel, name, outs, in_specs, flops=0, moved=0, grid=()):
    used = len(in_specs)

    def ordered(*refs):
        kernel(*refs[:used], *refs[used + 1 :])

    return pl.pallas_call(
        ordered,
        out_shape=outs,
        grid=grid,
        in_specs=in_specs + [pl.BlockSpec(memory_space=pl.ANY)],
        out_specs=[VMEM] * len(outs),
        compiler_params=pltpu.CompilerParams(vmem_limit_bytes=56 * 1024 * 1024),
        cost_estimate=pl.CostEstimate(flops=int(flops * COST[name]), bytes_accessed=moved if COST[name] > 0.5 else 0, transcendentals=0),
        name=name,
    )


def split_parts(value):
    first = value.astype(jnp.bfloat16)
    rest = value - first.astype(jnp.float32)
    second = rest.astype(jnp.bfloat16)
    third = (rest - second.astype(jnp.float32)).astype(jnp.bfloat16)
    return first, second, third


def store_meta(ref, pieces):
    tokens = pieces[0].shape[1]
    base = ref.shape[0] - META
    ref[base:, :] = jnp.zeros((META, ref.shape[1]), jnp.bfloat16)
    for number, piece in enumerate(pieces):
        piece = piece.astype(jnp.float32)
        missing = META - piece.shape[0]
        if missing:
            piece = jnp.concatenate([piece, jnp.zeros((missing, tokens), jnp.float32)], 0)
        ref[base:, number * tokens : (number + 1) * tokens] = piece.astype(jnp.bfloat16)


def load_meta(ref, tokens, number):
    base = ref.shape[0] - META
    return ref[base:, number * tokens : (number + 1) * tokens].astype(jnp.float32)


def join_kernel(tokens_ref, grad_ref, ids_ref, gates_ref, block_ref):
    tokens = tokens_ref.shape[0]
    block_ref[:tokens, :] = tokens_ref[...]
    block_ref[tokens : 2 * tokens, :] = grad_ref[...]
    store_meta(block_ref, (ids_ref[...].astype(jnp.float32).astype(jnp.bfloat16),) + split_parts(gates_ref[...]))


def selection(table_ref, block_ref, tokens, capacity, top):
    ids = load_meta(block_ref, tokens, 0)
    gates = load_meta(block_ref, tokens, 1) + load_meta(block_ref, tokens, 2) + load_meta(block_ref, tokens, 3)
    experts = [table_ref[place].astype(jnp.float32) for place in range(2 * CHIPS)]
    live = lax.broadcasted_iota(jnp.int32, ids.shape, 0) < top
    named = [(ids == expert) & live for expert in experts]
    hits = jnp.concatenate([jnp.sum(jnp.where(hit, 1.0, 0.0), 0, keepdims=True) for hit in named], 0)
    weights = [jnp.sum(jnp.where(hit, gates, 0.0), 0, keepdims=True) for hit in named]
    row = lax.broadcasted_iota(jnp.int32, (tokens, tokens), 0)
    column = lax.broadcasted_iota(jnp.int32, (tokens, tokens), 1)
    earlier = dot(hits.astype(jnp.bfloat16), jnp.where(row < column, 1.0, 0.0).astype(jnp.bfloat16))
    slot = lax.broadcasted_iota(jnp.int32, (capacity, tokens), 0).astype(jnp.float32)
    chosen = [
        jnp.where((slot == earlier[place : place + 1]) & (hits[place : place + 1] > 0.0), 1.0, 0.0)
        for place in range(2 * CHIPS)
    ]
    return chosen, weights, named


def pack_kernel(tokens, capacity, top, table_ref, block_ref, *out_refs):
    chosen, weights, _ = selection(table_ref, block_ref, tokens, capacity, top)
    stacked = jnp.concatenate(chosen, 0).astype(jnp.bfloat16)
    slot_gate = jnp.concatenate(
        [jnp.sum(pick * weight, 1, keepdims=True) for pick, weight in zip(chosen, weights)], 0
    )
    rows = dot(stacked, block_ref[:tokens, :]).astype(jnp.bfloat16)
    grads = (slot_gate * dot(stacked, block_ref[tokens : 2 * tokens, :])).astype(jnp.bfloat16)
    for place in range(2 * CHIPS):
        part = slice(place * capacity, (place + 1) * capacity)
        out_refs[place // 2][place % 2, :capacity, :] = rows[part]
        out_refs[place // 2][place % 2, capacity:, :] = grads[part]


def expert_kernel(capacity, *refs):
    in_refs, weight_refs, out_refs = refs[:CHIPS], refs[CHIPS : CHIPS + 6], refs[CHIPS + 6 : 2 * CHIPS + 6]
    rows_ref, grads_ref, act_ref, pre_gate_ref, pre_up_ref = refs[2 * CHIPS + 6 :]
    for core in range(2):
        gate_ref, up_ref, down_ref = weight_refs[3 * core : 3 * core + 3]
        rows = jnp.concatenate([ref[core, :capacity] for ref in in_refs], 0)
        grads = jnp.concatenate([ref[core, capacity:] for ref in in_refs], 0)
        rows_ref[core] = rows
        grads_ref[core] = grads
        pre_gate = dot(rows, gate_ref[...])
        pre_up = dot(rows, up_ref[...])
        sigmoid_gate = jax.nn.sigmoid(pre_gate)
        act = (pre_gate * sigmoid_gate * pre_up).astype(jnp.bfloat16)
        act_ref[core] = act
        out = dot(act, down_ref[...]).astype(jnp.bfloat16)
        grad_act = dot(grads, down_ref[...], TRAILING)
        grad_pre_gate = (
            grad_act * pre_up * sigmoid_gate * (1.0 + pre_gate * (1.0 - sigmoid_gate))
        ).astype(jnp.bfloat16)
        grad_pre_up = (grad_act * pre_gate * sigmoid_gate).astype(jnp.bfloat16)
        pre_gate_ref[core] = grad_pre_gate
        pre_up_ref[core] = grad_pre_up
        grad_in = (
            dot(grad_pre_gate, gate_ref[...], TRAILING) + dot(grad_pre_up, up_ref[...], TRAILING)
        ).astype(jnp.bfloat16)
        for chip in range(CHIPS):
            part = slice(chip * capacity, (chip + 1) * capacity)
            out_refs[chip][core, :capacity, :] = out[part]
            out_refs[chip][core, capacity:, :] = grad_in[part]


def merge_kernel(tokens, capacity, top, before, table_ref, block_ref, *refs):
    back_refs, earlier_refs, out_refs = refs[:CHIPS], refs[CHIPS : CHIPS + before], refs[CHIPS + before :]
    chosen, weights, named = selection(table_ref, block_ref, tokens, capacity, top)
    pieces = [ref[core] for ref in back_refs for core in range(2)]
    out = jnp.concatenate([piece[:capacity] for piece in pieces], 0)
    grad = jnp.concatenate([piece[capacity:] for piece in pieces], 0)
    stacked = jnp.concatenate(chosen, 0).astype(jnp.bfloat16)
    weighted = jnp.concatenate([pick * weight for pick, weight in zip(chosen, weights)], 0)
    high, low, _ = split_parts(weighted)
    mixed = dot(high, out, LEADING) + dot(low, out, LEADING)
    grad_in = dot(stacked, grad, LEADING)
    source = dot(stacked, block_ref[tokens : 2 * tokens, :])
    terms = jnp.sum(source * out.astype(jnp.float32), 1, keepdims=True)
    total = jnp.zeros(named[0].shape, jnp.float32)
    for place in range(2 * CHIPS):
        part = slice(place * capacity, (place + 1) * capacity)
        per_token = jnp.sum(chosen[place] * terms[part], 0, keepdims=True)
        total = total + jnp.where(named[place], per_token, 0.0)
    for ref in earlier_refs:
        mixed = mixed + ref[:tokens, :].astype(jnp.float32)
        grad_in = grad_in + ref[tokens : 2 * tokens, :].astype(jnp.float32)
        total = total + sum(load_meta(ref, tokens, number) for number in range(3))
    if len(out_refs) == 1:
        out_refs[0][:tokens, :] = mixed.astype(jnp.bfloat16)
        out_refs[0][tokens : 2 * tokens, :] = grad_in.astype(jnp.bfloat16)
        store_meta(out_refs[0], split_parts(total))
    else:
        out_refs[0][...] = mixed.astype(jnp.bfloat16)
        out_refs[1][...] = grad_in.astype(jnp.bfloat16)
        out_refs[2][...] = total[:top]


def weight_kernel(levels, *refs):
    steps = [refs[number : number + 5] for number in range(0, 5 * levels, 5)]
    gate_mat = sum(dot(rows[0], gate[0], LEADING) for rows, _, _, gate, _ in steps)
    up_mat = sum(dot(rows[0], up[0], LEADING) for rows, _, _, _, up in steps)
    down_mat = sum(dot(act[0], grads[0], LEADING) for _, grads, act, _, _ in steps)
    width, hidden = gate_mat.shape
    if len(refs) == 5 * levels + 1:
        refs[-1][:width, :hidden] = gate_mat.astype(jnp.bfloat16)
        refs[-1][:width, hidden:] = up_mat.astype(jnp.bfloat16)
        refs[-1][width:, :] = down_mat.astype(jnp.bfloat16)
        return
    other_ref, (gate_ref, up_ref, down_ref) = refs[5 * levels], refs[-3:]
    gate_ref[...] = (gate_mat + other_ref[:width, :hidden].astype(jnp.float32)).astype(jnp.bfloat16)
    up_ref[...] = (up_mat + other_ref[:width, hidden:].astype(jnp.float32)).astype(jnp.bfloat16)
    down_ref[...] = (down_mat + other_ref[width:, :].astype(jnp.float32)).astype(jnp.bfloat16)


def local_plane(tokens, expert_ids, gates, w_gate, w_up, w_down, grad_out):
    token_count, top_count = expert_ids.shape
    width = tokens.shape[1]
    hidden = w_gate.shape[2]
    axes = ("row", "col")
    plane = 2 * CHIPS
    device_count = lax.axis_size("row") * lax.axis_size("col")
    levels = device_count // plane
    average = token_count * top_count // device_count
    capacity = -(-min(token_count, average + average // 2) // 16) * 16
    me = lax.axis_index("row") * lax.axis_size("col") + lax.axis_index("col")
    table = (me // plane) * plane + jnp.bitwise_xor(me % plane, jnp.arange(plane, dtype=jnp.int32))
    bf16 = functools.partial(jax.ShapeDtypeStruct, dtype=jnp.bfloat16)

    def flip(value, mask):
        pairs = [(device, device ^ mask) for device in range(device_count)]
        return lax.ppermute(value, axes, pairs)

    def climb(value, step):
        pairs = [(device, (device + step * plane) % device_count) for device in range(device_count)]
        return lax.ppermute(value, axes, pairs)

    block_rows = 2 * token_count + META
    row_total = plane * capacity
    pair = bf16((2, 2 * capacity, width))
    half_rows = row_total // 2
    (block,) = call(join_kernel, "join", [bf16((block_rows, width))], [VMEM] * 4, 0, 4 * block_rows * width)(
        tokens, grad_out, expert_ids.T, gates.T, gates
    )
    order = sorted(range(levels), key=lambda step: min(step, levels - step))
    pack = call(
        functools.partial(pack_kernel, token_count, capacity, top_count),
        "pack",
        [pair] * CHIPS,
        [SMEM, VMEM],
        4 * row_total * token_count * width,
        2 * (block_rows + 2 * row_total) * width,
    )
    kept_shapes = [bf16((2, half_rows, size)) for size in (width, width, hidden, hidden, hidden)]
    expert = call(
        functools.partial(expert_kernel, capacity),
        "expert",
        [pair] * CHIPS + kept_shapes,
        [VMEM] * (CHIPS + 6),
        12 * row_total * width * hidden,
        2 * (6 * row_total * width + 3 * row_total * hidden + 6 * width * hidden),
    )
    half_block = bf16((token_count, width))
    results_shapes = [half_block, half_block, jax.ShapeDtypeStruct((top_count, token_count), jnp.float32)]

    def merge(before, final):
        return call(
            functools.partial(merge_kernel, token_count, capacity, top_count, before),
            "merge",
            results_shapes if final else [bf16((block_rows, width))],
            [SMEM] + [VMEM] * (1 + CHIPS + before),
            8 * row_total * token_count * width,
            2 * (2 * block_rows + 2 * row_total) * width,
        )

    def weight(core, partials):
        specs = [
            pl.BlockSpec((1,) + shape.shape[1:], lambda step: (core, 0, 0), memory_space=pltpu.VMEM) for shape in kept_shapes
        ]
        return call(
            functools.partial(weight_kernel, levels),
            "weight",
            [bf16((width, hidden)), bf16((width, hidden)), bf16((hidden, width))]
            if partials
            else [bf16((width + hidden, 2 * hidden))],
            specs * levels + [VMEM] * partials,
            3 * levels * row_total * width * hidden,
            levels * row_total * (2 * width + 3 * hidden) + 6 * width * hidden,
            (1,),
        )

    def after(value, *earlier):
        return lax.optimization_barrier((value,) + earlier)[0]

    moved = []

    def exchange(parts):
        earlier = moved[-BEHIND] if len(moved) >= BEHIND else None
        received = [parts[0]]
        for chip in range(1, CHIPS):
            part = after(parts[chip], *(earlier[1:] if STRICT else earlier[chip : chip + 1])) if earlier else parts[chip]
            received.append(flip(part, 2 * chip))
        moved.append(received)
        return received

    mats = [w_gate[0], w_up[0], w_down[0]]
    blocks = {0: block}
    for step in order[1:]:
        blocks[step] = climb(after(block, blocks[order[1]]) if CHAINZ and step == order[-2] else block, step)
    arrived, results, kept = {}, {}, {}
    last = block
    for turn in range(levels + AHEAD):
        if turn == min(WHEN, levels - 1):
            for mat in mats[:3]:
                mats.append(flip(mat, 1))
            last = after(last, *mats[3:])
        if turn < levels:
            packed = pack(table, blocks[order[turn]], last)
            last = packed[0]
            arrived[order[turn]] = exchange(packed)
        if turn >= AHEAD:
            step = order[turn - AHEAD]
            outs = expert(*arrived[step], *mats, last)
            last = outs[0]
            results[step], kept[step] = outs[:CHIPS], outs[CHIPS:]
    homeward = order[1:2] + order[:1:-1] + order[:1]
    returned = {step: exchange(results[step]) for step in homeward}
    saved = [value for step in order for value in kept[step]]
    sent = []
    for turn, step in enumerate(homeward):
        if turn == WPOS:
            (partial,) = weight(1, 0)(*saved, last)
            last = partial
            partial = flip(partial, 1)
        if turn == levels - 1:
            grad_mats = weight(0, 1)(*saved, partial, last)
            last = grad_mats[0]
        earlier, final = (sent, True) if step == 0 else ([], False)
        merged = merge(len(earlier), final)(table, blocks[step], *returned[step], *earlier, last)
        last = merged[0]
        if step:
            sent.append(climb(merged[0], levels - step))
    mixed, grad_tokens, grad_gates = merged
    return (mixed, grad_tokens, grad_gates.T) + tuple(mat[None] for mat in grad_mats)


def solution(mesh):
    return jax.shard_map(
        local_plane if plane_fits(mesh) else local_exchange,
        mesh=mesh,
        in_specs=(
            P(("groups", "row", "col"), "half"),
            P(("groups", "row", "col"), None),
            P(("groups", "row", "col"), None),
            P(("row", "col"), None, "half"),
            P(("row", "col"), None, "half"),
            P(("row", "col"), "half", None),
            P(("groups", "row", "col"), "half"),
        ),
        out_specs=(
            P(("groups", "row", "col"), "half"),
            P(("groups", "row", "col"), "half"),
            P(("groups", "row", "col"), None),
            P(("groups", "row", "col"), None, "half"),
            P(("groups", "row", "col"), None, "half"),
            P(("groups", "row", "col"), "half", None),
        ),
        check_vma=False,
    )
```
